256 devices in a mesh: img: 4 (over x), row: 8 (over z_hi, y), col: 8 (over z_lo, core).
Axes of the slice: x: 4, y: 4, z: 8 (z_hi: 2, z_lo: 4; z = z_hi * 4 + z_lo), core: 2. Of those that a mesh axis runs over, the one named last changes fastest.
Arguments:
- tokens: bfloat16 [4, 256, 128, 1152], P('img', 'row', 'col'), may hold values from -30 to 30
- qkv_weight: bfloat16 [1152, 1728], replicated, may hold values from -1 to 1
- out_weight: bfloat16 [1152, 576], replicated, may hold values from -0.25 to 0.25
- upstream: bfloat16 [4, 256, 128, 1152], P('img', 'row', 'col'), may hold values from -6 to 6
Outputs:
- sublayer_out: bfloat16 [4, 256, 128, 1152], P('img', 'row', 'col')
- tokens_grad: bfloat16 [4, 256, 128, 1152], P('img', 'row', 'col')
- qkv_grad: float32 [1152, 1728], P(('row', 'col'))
- out_grad: float32 [1152, 576], P(('row', 'col'))
The draws below stay inside these ranges and needn't reach their ends.
All inputs are finite; a program needn't handle non-finite values.
Results may differ from the reference program's by a relative error of at most 0.015.
Values may be sent and summed in bfloat16 or wider, within the bound.
A program may use at most 128 MiB of HBM per device.

```python
import jax
import jax.numpy as jnp
from jax import lax

D = 1152
H = 8
DH = 72
REACH = 8
WINDOW = 17
FRAME_ROWS = 256
FRAME_COLS = 128
IMAGES = 4


def draw_tokens(key, part):
    key = jax.random.fold_in(key, 11)
    first_key = jax.random.fold_in(key, 0)
    shape = (IMAGES, FRAME_ROWS, FRAME_COLS, D)
    values = jax.random.truncated_normal(first_key, -4.0, 4.0, shape, jnp.float32)
    return values.astype(jnp.bfloat16)


def draw_qkv_weight(key, part):
    key = jax.random.fold_in(key, 23)
    first_key = jax.random.fold_in(key, 0)
    inner = H * DH
    weights = jax.random.truncated_normal(first_key, -4.0, 4.0, (D, 3 * inner), jnp.float32) * D ** (-0.5)
    return weights.astype(jnp.bfloat16)


def levels(key, dims, pieces, least, largest):
    def one(axis_at, shards_of):
        steps = jax.random.uniform(jax.random.fold_in(jax.random.fold_in(key, 6), axis_at), (shards_of,), jnp.float32, least / len(pieces), largest / len(pieces))
        return jnp.repeat(jnp.exp(steps), dims[axis_at] // shards_of).reshape((-1,) + (1,) * (len(dims) - axis_at - 1))

    level = one(*pieces[0])
    for cut in pieces[1:]:
        level = level * one(*cut)
    return level


def gaussian(rng, shape, width, bound, cuts=(), held_as=jnp.bfloat16):
    factor_of = levels(rng, shape, cuts, -0.22, 0.18) if cuts else 1.0
    entries = jax.random.normal(rng, shape, jnp.float32) * width * factor_of
    return jnp.minimum(jnp.maximum(entries, -bound), bound).astype(held_as)


def setup_inputs(seed: int = 0) -> dict:
    arg_keys = jax.random.split(jax.random.key(seed), 5)
    tokens = draw_tokens(jax.random.fold_in(arg_keys[4], 71), 0)
    qkv_weight = draw_qkv_weight(jax.random.fold_in(arg_keys[4], 71), 0)
    out_weight = gaussian(arg_keys[2], (D, H * DH), (H * DH) ** -0.5, 0.25)
    upstream = gaussian(arg_keys[3], (IMAGES, FRAME_ROWS, FRAME_COLS, D), 1.0, 6.0, ((0, 4), (1, 8), (2, 8)))
    return dict(tokens=tokens, qkv_weight=qkv_weight, out_weight=out_weight, upstream=upstream)


band_step = 2

def clamp_starts(first_row, count, extent):
    places = first_row + jnp.arange(count, dtype=jnp.int32)
    return jnp.clip(places - REACH, 0, extent - WINDOW).astype(jnp.int32)

def reference(tokens, qkv_weight, out_weight, upstream):
    inner = H * DH
    scale = DH ** (-0.5)
    token_count = FRAME_ROWS * FRAME_COLS
    band_rows = band_step + 2 * REACH
    offsets = jnp.arange(WINDOW, dtype=jnp.int32)
    col_index = clamp_starts(0, FRAME_COLS, FRAME_COLS)[:, None] + offsets[None, :]
    qkv_total = jnp.zeros((D, 3 * inner), jnp.float32)
    out_total = jnp.zeros((D, inner), jnp.float32)
    results = []
    grads_in = []
    for image_idx in range(IMAGES):
        token_rows = tokens[image_idx].reshape(token_count, D)
        grad_rows = upstream[image_idx].reshape(token_count, D)
        projected = jnp.dot(token_rows, qkv_weight, preferred_element_type=jnp.float32).astype(jnp.bfloat16)
        projected = projected.reshape(FRAME_ROWS, FRAME_COLS, 3 * inner)
        grad_att = jnp.dot(grad_rows, out_weight, preferred_element_type=jnp.float32).astype(jnp.bfloat16)
        grad_att = grad_att.reshape(FRAME_ROWS, FRAME_COLS, inner)
        queries = projected[:, :, :inner]
        keys_all = projected[:, :, inner:2 * inner]
        values_all = projected[:, :, 2 * inner:]

        def block_step(carry, first_row):
            dkey_full, dvalue_full = carry
            band_start = jnp.clip(first_row - REACH, 0, FRAME_ROWS - band_rows).astype(jnp.int32)
            row_index = clamp_starts(first_row, band_step, FRAME_ROWS)[:, None] - band_start + offsets[None, :]

            def gather_window(field):
                col_taken = jnp.take(field, col_index, axis=1)
                row_taken = jnp.take(col_taken, row_index, axis=0)
                return row_taken.transpose(0, 2, 1, 3, 4).reshape(band_step * FRAME_COLS, WINDOW * WINDOW, H, DH)
            key_band = lax.dynamic_slice_in_dim(keys_all, band_start, band_rows, 0).astype(jnp.float32)
            value_band = lax.dynamic_slice_in_dim(values_all, band_start, band_rows, 0).astype(jnp.float32)
            key_win, scatter_back = jax.vjp(gather_window, key_band)
            value_win = gather_window(value_band)
            query_blk = lax.dynamic_slice_in_dim(queries, first_row, band_step, 0).astype(jnp.float32)
            query_blk = query_blk.reshape(band_step * FRAME_COLS, H, DH)
            grad_blk = lax.dynamic_slice_in_dim(grad_att, first_row, band_step, 0).astype(jnp.float32)
            grad_blk = grad_blk.reshape(band_step * FRAME_COLS, H, DH)
            scores = jnp.einsum('qhd,qkhd->qhk', query_blk, key_win) * scale
            row_max = lax.optimization_barrier(jnp.max(scores, axis=2, keepdims=True))
            shifted = jnp.exp(scores - row_max)
            attn_prob = shifted / lax.optimization_barrier(jnp.sum(shifted, axis=2, keepdims=True))
            prob_low = lax.optimization_barrier(attn_prob.astype(jnp.bfloat16)).astype(jnp.float32)
            attended = jnp.einsum('qhk,qkhd->qhd', prob_low, value_win)
            dprob = jnp.einsum('qhd,qkhd->qhk', grad_blk, value_win)
            row_dot = lax.optimization_barrier(jnp.sum(attn_prob * dprob, axis=2, keepdims=True))
            dscore = (attn_prob * (dprob - row_dot) * scale).astype(jnp.bfloat16)
            dscore = lax.optimization_barrier(dscore).astype(jnp.float32)
            dquery = jnp.einsum('qhk,qkhd->qhd', dscore, key_win)
            dkey_band = scatter_back(jnp.einsum('qhk,qhd->qkhd', dscore, query_blk))[0]
            dvalue_band = scatter_back(jnp.einsum('qhk,qhd->qkhd', prob_low, grad_blk))[0]
            dkey_full = lax.dynamic_update_slice_in_dim(dkey_full, lax.dynamic_slice_in_dim(dkey_full, band_start, band_rows, 0) + dkey_band, band_start, 0)
            dvalue_full = lax.dynamic_update_slice_in_dim(dvalue_full, lax.dynamic_slice_in_dim(dvalue_full, band_start, band_rows, 0) + dvalue_band, band_start, 0)
            return ((dkey_full, dvalue_full), (attended.astype(jnp.bfloat16).reshape(band_step * FRAME_COLS, inner), dquery.reshape(band_step * FRAME_COLS, inner)))
        firsts = jnp.arange(0, FRAME_ROWS, band_step, dtype=jnp.int32)
        zero_field = jnp.zeros((FRAME_ROWS, FRAME_COLS, inner), jnp.float32)
        (dkey_full, dvalue_full), (attended_blocks, dquery_blocks) = lax.scan(block_step, (zero_field, zero_field), firsts)
        attended = attended_blocks.reshape(token_count, inner)
        sublayer_out = jnp.dot(attended, out_weight.T, preferred_element_type=jnp.float32).astype(jnp.bfloat16)
        dqkv = jnp.concatenate([dquery_blocks.reshape(token_count, inner), dkey_full.reshape(token_count, inner), dvalue_full.reshape(token_count, inner)], axis=1).astype(jnp.bfloat16)
        tokens_grad = jnp.dot(dqkv, qkv_weight.T, preferred_element_type=jnp.float32).astype(jnp.bfloat16)
        qkv_total = qkv_total + jnp.dot(token_rows.T, dqkv, preferred_element_type=jnp.float32)
        out_total = out_total + jnp.dot(grad_rows.T, attended, preferred_element_type=jnp.float32)
        results.append(sublayer_out.reshape(FRAME_ROWS, FRAME_COLS, D))
        grads_in.append(tokens_grad.reshape(FRAME_ROWS, FRAME_COLS, D))
    return (jnp.stack(results), jnp.stack(grads_in), qkv_total, out_total)
```

```python
import functools

import jax
import jax.numpy as jnp
from jax import lax
from jax.experimental import pallas as pl
from jax.experimental.pallas import tpu as pltpu
from jax.sharding import PartitionSpec as P

H = 8
DH = 72
REACH = 8
WINDOW = 17
INNER = H * DH
PAIRS = H // 2
SPAN = 256
WIDE = 640
SHIFT = 64

masked_score = -1e30
bf16 = jnp.bfloat16
f32 = jnp.float32
MESH = pl.DeviceIdType.MESH
VMEM_SPEC = pl.BlockSpec(memory_space=pltpu.VMEM)
ANY_SPEC = pl.BlockSpec(memory_space=pl.ANY)


def mm(a, b):
    return jnp.dot(a, b, preferred_element_type=f32)


def by_column_block(rows):
    count, width = rows.shape
    parts = rows.reshape(count // 16, 2, 8, width)
    return [parts[:, j].reshape(count // 2, width) for j in range(2)]


def project_kernel(tok_ref, up_ref, wqkv_ref, wout_ref, q_ref, kv_ref, ga_ref):
    x = tok_ref[...]
    query = by_column_block(mm(x, wqkv_ref[:, :WIDE]))
    key = by_column_block(mm(x, wqkv_ref[:, 512 : 2 * INNER])[:, SHIFT:])
    value = by_column_block(mm(x, wqkv_ref[:, 2 * INNER :]))
    for j in range(2):
        q_ref[j] = query[j].astype(bf16)
        kv_ref[j] = jnp.concatenate([key[j], value[j]], axis=1).astype(bf16)
    grads = by_column_block(mm(up_ref[...], wout_ref[...]))
    for j in range(2):
        blank = jnp.zeros((grads[j].shape[0], SHIFT), f32)
        ga_ref[j] = jnp.concatenate([blank, grads[j]], axis=1).astype(bf16)


def project(token_rows, grad_rows, qkv_weight, out_weight):
    half = token_rows.shape[0] // 2
    return pl.pallas_call(
        project_kernel,
        out_shape=(
            jax.ShapeDtypeStruct((2, half, WIDE), bf16),
            jax.ShapeDtypeStruct((2, half, 2 * INNER), bf16),
            jax.ShapeDtypeStruct((2, half, WIDE), bf16),
        ),
        in_specs=[VMEM_SPEC] * 4,
        out_specs=(VMEM_SPEC,) * 3,
        compiler_params=pltpu.CompilerParams(vmem_limit_bytes=48 * 2**20),
        name="project",
    )(token_rows, grad_rows, qkv_weight, out_weight)


AROUND = [(dr, dc) for dr in (-1, 0, 1) for dc in (-1, 0, 1) if (dr, dc) != (0, 0)]


def halo_part(dr, dc):
    blocks = {-1: slice(0, 1), 0: slice(1, 3), 1: slice(3, 4)}[dc]
    tokens = {-1: slice(0, 64), 0: slice(64, 320), 1: slice(320, 384)}[dr]
    return blocks, tokens


def owned_part(dr, dc):
    blocks = {-1: slice(1, 2), 0: slice(0, 2), 1: slice(0, 1)}[dc]
    tokens = {-1: slice(192, 256), 0: slice(0, 256), 1: slice(0, 64)}[dr]
    return blocks, tokens


def size_of(part):
    return tuple(s.stop - s.start for s in part)


def place():
    return lax.axis_index("row"), lax.axis_index("col")


def inside(row, col):
    rows, cols = lax.axis_size("row"), lax.axis_size("col")
    return (row >= 0) & (row < rows) & (col >= 0) & (col < cols)


def greet_around(row, col):
    barrier = pltpu.get_barrier_semaphore()
    count = jnp.int32(0)
    for dr, dc in AROUND:
        there = inside(row + dr, col + dc)
        count = count + there.astype(jnp.int32)

        @pl.when(there)
        def _():
            pl.semaphore_signal(
                barrier,
                inc=1,
                device_id={"row": row + dr, "col": col + dc},
                device_id_type=MESH,
            )

    pl.semaphore_wait(barrier, count)


def halo_kernel(kv_ref, ext_ref, zeros, send_sem, recv_sem, local_sem):
    row, col = place()
    greet_around(row, col)

    def sending(n):
        dr, dc = AROUND[n]
        return pltpu.make_async_remote_copy(
            src_ref=kv_ref.at[owned_part(dr, dc)],
            dst_ref=ext_ref.at[halo_part(dr, dc)],
            send_sem=send_sem.at[n],
            recv_sem=recv_sem.at[n],
            device_id={"row": row - dr, "col": col - dc},
            device_id_type=MESH,
        )

    for n, (dr, dc) in enumerate(AROUND):

        @pl.when(inside(row - dr, col - dc))
        def _():
            sending(n).start()

    own = pltpu.make_async_copy(kv_ref, ext_ref.at[1:3, 64:320], local_sem.at[8])
    own.start()
    zeros[...] = jnp.zeros_like(zeros)

    def blanking(n):
        part = halo_part(*AROUND[n])
        blocks, tokens = size_of(part)
        return pltpu.make_async_copy(
            zeros.at[:blocks, :tokens], ext_ref.at[part], local_sem.at[n]
        )

    for n, (dr, dc) in enumerate(AROUND):

        @pl.when(jnp.logical_not(inside(row + dr, col + dc)))
        def _():
            blanking(n).start()

    for n, (dr, dc) in enumerate(AROUND):

        @pl.when(inside(row + dr, col + dc))
        def _():
            sending(n).wait_recv()

        @pl.when(jnp.logical_not(inside(row + dr, col + dc)))
        def _():
            blanking(n).wait()

    for n, (dr, dc) in enumerate(AROUND):

        @pl.when(inside(row - dr, col - dc))
        def _():
            sending(n).wait_send()

    own.wait()


def with_halo(kv):
    return pl.pallas_call(
        halo_kernel,
        out_shape=jax.ShapeDtypeStruct((4, 384, 2 * INNER), bf16),
        in_specs=[ANY_SPEC],
        out_specs=ANY_SPEC,
        scratch_shapes=[
            pltpu.VMEM((2, 256, 2 * INNER), bf16),
            pltpu.SemaphoreType.DMA((8,)),
            pltpu.SemaphoreType.DMA((8,)),
            pltpu.SemaphoreType.DMA((9,)),
        ],
        compiler_params=pltpu.CompilerParams(collective_id=0, has_side_effects=True),
        name="halo",
    )(kv)


def attention_kernel(
    cols_bound, rows_bound, ext_ref, q_ref, ga_ref, att_ref, dq_ref, dkv_ref,
    grads, k_turned, v_turned, bias, att_sum, dq_sum,
):
    row, col = place()
    row_first, col_first = row * 32, col * 16
    last_col = lax.axis_size("col") - 1
    exp_scale = DH ** (-0.5) * 1.4426950408889634

    for p in range(PAIRS):
        for cb in range(4):
            k_turned[p, cb] = ext_ref[cb, :, pl.ds(128 * p, SPAN)].T
            v_turned[p, cb] = ext_ref[cb, :, pl.ds(512 + 128 * p, SPAN)].T
    grads[...] = jnp.zeros_like(grads)
    att_sum[...] = jnp.zeros_like(att_sum)
    dq_sum[...] = jnp.zeros_like(dq_sum)

    at_row = lax.broadcasted_iota(jnp.int32, (SPAN, 128), 0)
    at_lane = lax.broadcasted_iota(jnp.int32, (128, SPAN), 1)

    def head_of(at, first):
        return (at >= first) & (at < first + DH)

    def split_turned(block, first):
        turned = block.T
        none = jnp.zeros_like(turned)
        return jnp.concatenate(
            [jnp.where(head_of(at_row, first + n * DH), turned, none) for n in range(2)], axis=1
        )

    def split_rows(block, first):
        none = jnp.zeros_like(block)
        return jnp.concatenate(
            [jnp.where(head_of(at_lane, first + n * DH), block, none) for n in range(2)], axis=0
        )

    def joined(turned, first):
        kept = jnp.where(
            head_of(at_row, first),
            turned[:, :128],
            jnp.where(head_of(at_row, first + DH), turned[:, 128:], 0.0),
        )
        return kept.T.reshape(16, 8, SPAN)

    def strip(s, _):
        j, t = s // 2, s % 2
        first_cb = jnp.where(col == 0, 1, jnp.where(col == last_col, 0, j))
        at = pl.multiple_of(128 * t, 128)
        band = pl.ds(at, 256)
        key_at = lax.broadcasted_iota(jnp.int32, (256, 128), 0)
        query_at = lax.broadcasted_iota(jnp.int32, (256, 128), 1)
        query_row = row_first + 16 * t + query_at // 8
        query_col = col_first + 8 * j + query_at % 8
        row_start = jnp.clip(query_row - REACH, 0, rows_bound)
        col_start = jnp.clip(query_col - REACH, 0, cols_bound)
        for b in range(3):
            key_row = row_first + 16 * t - REACH + key_at // 8
            key_col = col_first + 8 * (first_cb + b) - REACH + key_at % 8
            seen = (
                (key_row >= row_start)
                & (key_row <= row_start + 2 * REACH)
                & (key_col >= col_start)
                & (key_col <= col_start + 2 * REACH)
            )
            bias[b] = jnp.where(seen, 0.0, masked_score)
        for p in range(PAIRS):
            low, high = 16 * p, SHIFT + 16 * p
            here = pl.ds(128 * p, SPAN)
            there = pl.ds(512 + 128 * p, SPAN)
            query = q_ref[j, pl.ds(at, 128), here]
            upward = ga_ref[j, pl.ds(at, 128), here]
            query_turned = split_turned(query, low)
            upward_turned = split_turned(upward, high)
            scores = []
            for b in range(3):
                hidden = bias[b]
                scores.append(
                    mm(ext_ref[first_cb + b, band, here], query_turned)
                    + jnp.concatenate([hidden, hidden], axis=1)
                )
            top = functools.reduce(
                jnp.maximum, [jnp.max(x, axis=0, keepdims=True) for x in scores]
            )
            shifted = [jnp.exp2((x - top) * exp_scale) for x in scores]
            total = sum(jnp.sum(x, axis=0, keepdims=True) for x in shifted)
            inverse = 1.0 / total
            prob = [x * inverse for x in shifted]
            prob_low = [x.astype(bf16) for x in prob]
            dprob = [mm(ext_ref[first_cb + b, band, there], upward_turned) for b in range(3)]
            row_dot = sum(
                jnp.sum(x * y, axis=0, keepdims=True) for x, y in zip(prob, dprob)
            )
            dscore = [(x * (y - row_dot)).astype(bf16) for x, y in zip(prob, dprob)]
            att = sum(mm(v_turned[p, first_cb + b, :, band], prob_low[b]) for b in range(3))
            dquery = sum(mm(k_turned[p, first_cb + b, :, band], dscore[b]) for b in range(3))
            rows = pl.ds(16 * t, 16)
            att_sum[rows, j, :, here] += joined(att, high)
            dq_sum[rows, j, :, here] += joined(dquery, low)
            query_rows = split_rows(query, low)
            upward_rows = split_rows(upward, high)
            for b in range(3):
                grads[first_cb + b, band, here] += mm(dscore[b], query_rows)
                grads[first_cb + b, band, there] += mm(prob_low[b], upward_rows)
        return 0

    lax.fori_loop(0, 4, strip, 0)
    scale = DH ** (-0.5)
    att_ref[...] = att_sum[...].reshape(att_ref.shape).astype(bf16)
    dq_ref[...] = (dq_sum[...] * scale).reshape(dq_ref.shape).astype(bf16)
    for cb in range(4):
        dkv_ref[cb, :, :INNER] = (grads[cb, :, :INNER] * scale).astype(bf16)
        dkv_ref[cb, :, INNER:] = grads[cb, :, INNER:].astype(bf16)


def attention(ext, query, grad_att):
    rows = 32 * lax.axis_size("row")
    cols = 16 * lax.axis_size("col")
    tokens = 2 * query.shape[1]
    return pl.pallas_call(
        functools.partial(attention_kernel, cols - WINDOW, rows - WINDOW),
        out_shape=(
            jax.ShapeDtypeStruct((tokens, WIDE), bf16),
            jax.ShapeDtypeStruct((tokens, WIDE), bf16),
            jax.ShapeDtypeStruct(ext.shape, bf16),
        ),
        in_specs=[VMEM_SPEC] * 3,
        out_specs=(VMEM_SPEC,) * 3,
        scratch_shapes=[
            pltpu.VMEM(ext.shape, f32),
            pltpu.VMEM((PAIRS, 4, SPAN, 384), bf16),
            pltpu.VMEM((PAIRS, 4, SPAN, 384), bf16),
            pltpu.VMEM((3, 256, 128), f32),
            pltpu.VMEM((32, 2, 8, WIDE), f32),
            pltpu.VMEM((32, 2, 8, WIDE), f32),
        ],
        compiler_params=pltpu.CompilerParams(vmem_limit_bytes=56 * 2**20),
        name="attention",
    )(ext, query, grad_att)


def return_kernel(dkv_ref, out_ref, side, flat, corner, total, send_sem, recv_sem):
    row, col = place()
    greet_around(row, col)
    slots = {}
    for n, (dr, dc) in enumerate(AROUND):
        if dr == 0:
            slots[n] = side.at[pl.ds((dc + 1) // 2, 1)]
        elif dc == 0:
            slots[n] = flat.at[(dr + 1) // 2]
        else:
            slots[n] = corner.at[pl.ds(dr + 1 + (dc + 1) // 2, 1)]

    def sending(n):
        dr, dc = AROUND[n]
        return pltpu.make_async_remote_copy(
            src_ref=dkv_ref.at[halo_part(dr, dc)],
            dst_ref=slots[n],
            send_sem=send_sem.at[n],
            recv_sem=recv_sem.at[n],
            device_id={"row": row + dr, "col": col + dc},
            device_id_type=MESH,
        )

    for n, (dr, dc) in enumerate(AROUND):

        @pl.when(inside(row + dr, col + dc))
        def _():
            sending(n).start()

    total[...] = dkv_ref[1:3, 64:320].astype(f32)
    for n, (dr, dc) in enumerate(AROUND):

        @pl.when(inside(row - dr, col - dc))
        def _():
            sending(n).wait_recv()
            total[owned_part(dr, dc)] += slots[n][...].astype(f32)

    mine = total[...].reshape(2, 32, 8, 2 * INNER)
    for j in range(2):
        out_ref[:, j] = mine[j]

    for n, (dr, dc) in enumerate(AROUND):

        @pl.when(inside(row + dr, col + dc))
        def _():
            sending(n).wait_send()


def returned(dkv):
    out = pl.pallas_call(
        return_kernel,
        out_shape=jax.ShapeDtypeStruct((32, 2, 8, 2 * INNER), f32),
        in_specs=[VMEM_SPEC],
        out_specs=VMEM_SPEC,
        scratch_shapes=[
            pltpu.VMEM((2, 256, 2 * INNER), bf16),
            pltpu.VMEM((2, 2, 64, 2 * INNER), bf16),
            pltpu.VMEM((4, 64, 2 * INNER), bf16),
            pltpu.VMEM((2, 256, 2 * INNER), f32),
            pltpu.SemaphoreType.DMA((8,)),
            pltpu.SemaphoreType.DMA((8,)),
        ],
        compiler_params=pltpu.CompilerParams(
            collective_id=1, has_side_effects=True, vmem_limit_bytes=40 * 2**20
        ),
        name="give_back",
    )(dkv)
    return out.reshape(512, 2 * INNER).astype(bf16)


def weight_kernel(tok_ref, up_ref, dq_ref, dkv_ref, att_ref, g_ref, turned):
    turned[0] = tok_ref[...].T
    turned[1] = up_ref[...].T

    def rows(n, _):
        at = pl.ds(pl.multiple_of(n * 288, 16), 288)
        for g in range(4):
            left = turned[1 if g == 3 else 0, at, :]
            right = (
                dq_ref[...],
                dkv_ref[:, :WIDE],
                dkv_ref[:, 2 * INNER - WIDE :],
                att_ref[...],
            )[g]
            g_ref[pl.ds(2 * n, 2), g] = mm(left, right).reshape(2, 144, WIDE).astype(bf16)
        return 0

    lax.fori_loop(0, 4, rows, 0)


def weight_grads(token_rows, grad_rows, dq, dkv, att):
    tokens, width = token_rows.shape
    return pl.pallas_call(
        weight_kernel,
        out_shape=jax.ShapeDtypeStruct((8, 4, 144, WIDE), bf16),
        in_specs=[VMEM_SPEC] * 5,
        out_specs=VMEM_SPEC,
        scratch_shapes=[pltpu.VMEM((2, width, tokens), bf16)],
        compiler_params=pltpu.CompilerParams(vmem_limit_bytes=48 * 2**20),
        name="weight_grads",
    )(token_rows, grad_rows, dq, dkv, att)


UPPER = 80


def sum_kernel(
    g_ref, out_ref, mine, recv0, rx1, ry1, a1, a2, rx2, ry2, b, rz, w, fin,
    sem0, sem_x1, sem_y1, sem_x2, sem_y2, send_z, recv_z, send_f, recv_f, local_sem,
):
    img = lax.axis_index("img")
    row, col = place()
    z_hi, y = row // 4, row % 4
    z_lo, core = col // 2, col % 2
    z = z_hi * 4 + z_lo
    other = 1 - core

    def device(img=img, z_hi=z_hi, y=y, z_lo=z_lo, core=core):
        return {"img": img, "row": z_hi * 4 + y, "col": z_lo * 2 + core}

    barrier = pltpu.get_barrier_semaphore()
    greeted = [device(core=other)]
    greeted += [device(img=(img + d) % 4) for d in range(1, 4)]
    greeted += [device(img=(img + d) % 4, core=other) for d in range(1, 4)]
    greeted += [device(y=(y + d) % 4) for d in range(1, 4)]
    for d in range(1, 8):
        z_there = (z + d) % 8
        greeted.append(device(z_hi=z_there // 4, z_lo=z_there % 4))
    for target in greeted:
        pl.semaphore_signal(barrier, inc=1, device_id=target, device_id_type=MESH)
    pl.semaphore_wait(barrier, len(greeted))

    def remote(src, dst, send, recv, target):
        return pltpu.make_async_remote_copy(
            src_ref=src, dst_ref=dst, send_sem=send, recv_sem=recv,
            device_id=target, device_id_type=MESH,
        )

    swaps, loads = [], []
    for k in range(4):
        swaps.append(
            remote(g_ref.at[other, k], recv0.at[k], sem0.at[0, k], sem0.at[1, k], device(core=other))
        )
        loads.append(pltpu.make_async_copy(g_ref.at[core, k], mine.at[k], local_sem.at[k]))
        swaps[k].start()
        loads[k].start()
    for k in range(4):
        loads[k].wait()
        swaps[k].wait_recv()

        def add(n, _):
            mine[k, n] = (mine[k, n].astype(f32) + recv0[k, n].astype(f32)).astype(bf16)
            return 0

        lax.fori_loop(0, 4, add, 0)

    first = []
    for d in range(1, 4):
        x_there, y_there = (img + d) % 4, (y + d) % 4
        first.append(
            remote(
                mine.at[:, x_there, :UPPER], rx1.at[d - 1],
                sem_x1.at[0, d - 1], sem_x1.at[1, d - 1], device(img=x_there),
            )
        )
        first.append(
            remote(
                mine.at[y_there, :, UPPER:], ry1.at[d - 1],
                sem_y1.at[0, d - 1], sem_y1.at[1, d - 1], device(y=y_there),
            )
        )
    for copy in first:
        copy.start()
    for copy in first:
        copy.wait_recv()

    def add_first(n, _):
        upper = mine[n, img, :UPPER].astype(f32)
        lower = mine[y, n, UPPER:].astype(f32)
        for d in range(3):
            upper += rx1[d, n].astype(f32)
            lower += ry1[d, n].astype(f32)
        a1[n] = upper.astype(bf16)
        a2[n] = lower.astype(bf16)
        return 0

    lax.fori_loop(0, 4, add_first, 0)

    second = []
    for d in range(1, 4):
        x_there, y_there = (img + d) % 4, (y + d) % 4
        second.append(
            remote(
                a1.at[y_there], ry2.at[d - 1],
                sem_y2.at[0, d - 1], sem_y2.at[1, d - 1], device(y=y_there),
            )
        )
        second.append(
            remote(
                a2.at[x_there], rx2.at[d - 1],
                sem_x2.at[0, d - 1], sem_x2.at[1, d - 1], device(img=x_there),
            )
        )
    for copy in second:
        copy.start()
    for copy in second:
        copy.wait_recv()
    upper = a1[y].astype(f32)
    lower = a2[img].astype(f32)
    for d in range(3):
        upper += ry2[d].astype(f32)
        lower += rx2[d].astype(f32)
    b[:UPPER] = upper.astype(bf16)
    b[UPPER:] = lower.astype(bf16)

    holder = z_hi == core

    def to_chip(n):
        return remote(
            b.at[pl.ds(32 * n, 48)], rz.at[z], send_z.at[n], recv_z.at[z],
            device(z_hi=core, z_lo=n),
        )

    def from_chip(n):
        return remote(
            b.at[pl.ds(0, 48)], rz.at[n], send_z.at[0], recv_z.at[n], device(core=other)
        )

    for n in range(4):

        @pl.when(jnp.logical_not(holder & (z_lo == n)))
        def _():
            to_chip(n).start()

    def to_owner(d, k):
        return remote(
            w.at[pl.ds(16 * k, 32)], fin.at[img], send_f.at[d, k], recv_f.at[img],
            device(img=(img + d) % 4, core=k),
        )

    @pl.when(holder)
    def _():
        for n in range(8):

            @pl.when(z != n)
            def _():
                from_chip(n).wait_recv()

        own = b[pl.ds(pl.multiple_of(32 * z_lo, 32), 48)].astype(f32)
        rz[z] = own.astype(bf16)
        added = rz[0].astype(f32)
        for n in range(1, 8):
            added += rz[n].astype(f32)
        w[...] = added.astype(bf16)
        for d in range(4):
            for k in range(2):

                @pl.when((core != k) | (d != 0))
                def _():
                    to_owner(d, k).start()

        kept = pltpu.make_async_copy(
            w.at[pl.ds(pl.multiple_of(16 * core, 16), 32)], fin.at[img], local_sem.at[4]
        )
        kept.start()
        kept.wait()

    def from_holder(n):
        return remote(
            w.at[pl.ds(0, 32)], fin.at[n], send_f.at[0, 0], recv_f.at[n], device(core=other)
        )

    for n in range(4):

        @pl.when(jnp.logical_not(holder) | (img != n))
        def _():
            from_holder(n).wait_recv()

    out_ref[...] = fin[...]

    for copy in swaps + first + second:
        copy.wait_send()
    for n in range(4):

        @pl.when(jnp.logical_not(holder & (z_lo == n)))
        def _():
            to_chip(n).wait_send()

    @pl.when(holder)
    def _():
        for d in range(4):
            for k in range(2):

                @pl.when((core != k) | (d != 0))
                def _():
                    to_owner(d, k).wait_send()


def sum_over_devices(g):
    rest = UPPER, 144 - UPPER
    dma = pltpu.SemaphoreType.DMA
    return pl.pallas_call(
        sum_kernel,
        out_shape=jax.ShapeDtypeStruct((4, 32, WIDE), bf16),
        in_specs=[ANY_SPEC],
        out_specs=VMEM_SPEC,
        scratch_shapes=[
            pltpu.VMEM((4, 4, 144, WIDE), bf16),
            pltpu.VMEM((4, 4, 144, WIDE), bf16),
            pltpu.VMEM((3, 4, rest[0], WIDE), bf16),
            pltpu.VMEM((3, 4, rest[1], WIDE), bf16),
            pltpu.VMEM((4, rest[0], WIDE), bf16),
            pltpu.VMEM((4, rest[1], WIDE), bf16),
            pltpu.VMEM((3, rest[1], WIDE), bf16),
            pltpu.VMEM((3, rest[0], WIDE), bf16),
            pltpu.VMEM((144, WIDE), bf16),
            pltpu.VMEM((8, 48, WIDE), bf16),
            pltpu.VMEM((48, WIDE), bf16),
            pltpu.VMEM((4, 32, WIDE), bf16),
            dma((2, 4)),
            dma((2, 3)),
            dma((2, 3)),
            dma((2, 3)),
            dma((2, 3)),
            dma((4,)),
            dma((8,)),
            dma((4, 2)),
            dma((4,)),
            dma((5,)),
        ],
        compiler_params=pltpu.CompilerParams(
            collective_id=2, has_side_effects=True, vmem_limit_bytes=40 * 2**20
        ),
        name="sum_over_devices",
    )(g.reshape(2, 4, 4, 144, WIDE))


def local(tokens, qkv_weight, out_weight, upstream):
    count = tokens.shape[1] * tokens.shape[2]
    width = tokens.shape[3]
    token_rows = tokens.reshape(count, width)
    grad_rows = upstream.reshape(count, width)
    query, keyvals, grad_att = project(token_rows, grad_rows, qkv_weight, out_weight)
    extended = with_halo(keyvals)
    att, dq, dkv = attention(extended, query, grad_att)
    nt = (((1,), (1,)), ((), ()))
    sublayer_out = lax.dot_general(
        att[:, SHIFT:], out_weight, nt, preferred_element_type=f32
    ).astype(bf16)
    dkv = returned(dkv)
    dqkv = jnp.concatenate([dq[:, :INNER], dkv], axis=1)
    tokens_grad = lax.dot_general(dqkv, qkv_weight, nt, preferred_element_type=f32).astype(bf16)
    shares = sum_over_devices(weight_grads(token_rows, grad_rows, dq, dkv, att))
    shares = lax.dynamic_slice_in_dim(shares, 2 * lax.axis_index("col"), 18, 1).astype(f32)
    qkv_grad = jnp.concatenate(
        [shares[0, :, :INNER], shares[1, :, :INNER], shares[2, :, SHIFT:]], axis=1
    )
    return (
        sublayer_out.reshape(tokens.shape),
        tokens_grad.reshape(tokens.shape),
        qkv_grad,
        shares[3, :, SHIFT:],
    )


def solution(mesh):
    return jax.shard_map(
        local,
        mesh=mesh,
        in_specs=(P("img", "row", "col", None), P(), P(), P("img", "row", "col", None)),
        out_specs=(
            P("img", "row", "col", None),
            P("img", "row", "col", None),
            P(("row", "col"), None),
            P(("row", "col"), None),
        ),
        check_vma=False,
    )
```

```python
import functools

import jax
import jax.numpy as jnp
from jax import lax
from jax.experimental import pallas as pl
from jax.experimental.pallas import tpu as pltpu
from jax.sharding import PartitionSpec as P

H = 8
DH = 72
REACH = 8
WINDOW = 17
INNER = H * DH
PAIRS = H // 2
SPAN = 256
WIDE = 640
SHIFT = 64

masked_score = -1e30
bf16 = jnp.bfloat16
f32 = jnp.float32
MESH = pl.DeviceIdType.MESH
VMEM_SPEC = pl.BlockSpec(memory_space=pltpu.VMEM)
ANY_SPEC = pl.BlockSpec(memory_space=pl.ANY)


def mm(a, b):
    return jnp.dot(a, b, preferred_element_type=f32)


def mm_nt(a, b):
    return lax.dot_general(a, b, (((1,), (1,)), ((), ())), preferred_element_type=f32)


def by_column_block(rows):
    count, width = rows.shape
    parts = rows.reshape(count // 16, 2, 8, width)
    return [parts[:, j].reshape(count // 2, width) for j in range(2)]


def project_kernel(tok_ref, up_ref, wqkv_ref, wout_ref, q_ref, kv_ref, ga_ref):
    x = tok_ref[...]
    query = by_column_block(mm_nt(x, wqkv_ref[:WIDE]))
    key = by_column_block(mm_nt(x, wqkv_ref[INNER : 2 * INNER]))
    value = by_column_block(mm_nt(x, wqkv_ref[2 * INNER :]))
    for j in range(2):
        q_ref[j] = query[j].astype(bf16)
        kv_ref[j] = jnp.concatenate([key[j], value[j]], axis=1).astype(bf16)
    grads = by_column_block(mm_nt(up_ref[...], wout_ref[...]))
    for j in range(2):
        blank = jnp.zeros((grads[j].shape[0], SHIFT), f32)
        ga_ref[j] = jnp.concatenate([blank, grads[j]], axis=1).astype(bf16)


def project(token_rows, grad_rows, qkv_weight, out_weight):
    half = token_rows.shape[0] // 2
    return pl.pallas_call(
        project_kernel,
        out_shape=(
            jax.ShapeDtypeStruct((2, half, WIDE), bf16),
            jax.ShapeDtypeStruct((2, half, 2 * INNER), bf16),
            jax.ShapeDtypeStruct((2, half, WIDE), bf16),
        ),
        in_specs=[VMEM_SPEC] * 4,
        out_specs=(VMEM_SPEC,) * 3,
        compiler_params=pltpu.CompilerParams(vmem_limit_bytes=28 * 2**20),
        name="project",
    )(token_rows, grad_rows, qkv_weight, out_weight)


AROUND = [(dr, dc) for dr in (-1, 0, 1) for dc in (-1, 0, 1) if (dr, dc) != (0, 0)]


def halo_part(dr, dc):
    blocks = {-1: slice(0, 1), 0: slice(1, 3), 1: slice(3, 4)}[dc]
    tokens = {-1: slice(0, 64), 0: slice(64, 320), 1: slice(320, 384)}[dr]
    return blocks, tokens


def owned_part(dr, dc):
    blocks = {-1: slice(1, 2), 0: slice(0, 2), 1: slice(0, 1)}[dc]
    tokens = {-1: slice(192, 256), 0: slice(0, 256), 1: slice(0, 64)}[dr]
    return blocks, tokens


def size_of(part):
    return tuple(s.stop - s.start for s in part)


def place():
    return lax.axis_index("row"), lax.axis_index("col")


def inside(row, col):
    rows, cols = lax.axis_size("row"), lax.axis_size("col")
    return (row >= 0) & (row < rows) & (col >= 0) & (col < cols)


BESIDE = [(-1, 0), (1, 0), (0, -1), (0, 1)]


def greet_beside(row, col):
    barrier = pltpu.get_barrier_semaphore()
    count = jnp.int32(0)
    for dr, dc in BESIDE:
        there = inside(row + dr, col + dc)
        count = count + there.astype(jnp.int32)

        @pl.when(there)
        def _():
            pl.semaphore_signal(
                barrier,
                inc=1,
                device_id={"row": row + dr, "col": col + dc},
                device_id_type=MESH,
            )

    pl.semaphore_wait(barrier, count)


def halo_kernel(kv_ref, ext_ref, send_sem, recv_sem):
    row, col = place()
    greet_beside(row, col)

    def sending(n):
        dr, dc = AROUND[n]
        blocks, tokens = halo_part(dr, dc)
        if dr == 0 or dc == 0:
            src = kv_ref.at[owned_part(dr, dc)]
            target = {"row": row - dr, "col": col - dc}
        else:
            src = ext_ref.at[{-1: slice(2, 3), 1: slice(1, 2)}[dc], tokens]
            target = {"row": row, "col": col - dc}
        return pltpu.make_async_remote_copy(
            src_ref=src,
            dst_ref=ext_ref.at[blocks, tokens],
            send_sem=send_sem.at[n],
            recv_sem=recv_sem.at[n],
            device_id=target,
            device_id_type=MESH,
        )

    def sends(dr, dc):
        if dr == 0 or dc == 0:
            return inside(row - dr, col - dc)
        return inside(row + dr, col) & inside(row, col - dc)

    index = {way: n for n, way in enumerate(AROUND)}
    for dr, dc in BESIDE:

        @pl.when(sends(dr, dc))
        def _():
            sending(index[dr, dc]).start()

    ext_ref[1:3, 64:320] = kv_ref[...]

    for n, (dr, dc) in enumerate(AROUND):

        @pl.when(jnp.logical_not(inside(row + dr, col + dc)))
        def _():
            part = halo_part(dr, dc)
            ext_ref[part] = jnp.zeros(size_of(part) + (2 * INNER,), bf16)

    for dr in (-1, 1):

        @pl.when(inside(row + dr, col))
        def _():
            sending(index[dr, 0]).wait_recv()

        for dc in (-1, 1):

            @pl.when(sends(dr, dc))
            def _():
                sending(index[dr, dc]).start()

    for n, (dr, dc) in enumerate(AROUND):
        if dc != 0:

            @pl.when(inside(row + dr, col + dc))
            def _():
                sending(n).wait_recv()

    for n, (dr, dc) in enumerate(AROUND):

        @pl.when(sends(dr, dc))
        def _():
            sending(n).wait_send()


def with_halo(kv):
    return pl.pallas_call(
        halo_kernel,
        out_shape=jax.ShapeDtypeStruct((4, 384, 2 * INNER), bf16),
        in_specs=[VMEM_SPEC],
        out_specs=VMEM_SPEC,
        scratch_shapes=[
            pltpu.SemaphoreType.DMA((8,)),
            pltpu.SemaphoreType.DMA((8,)),
        ],
        compiler_params=pltpu.CompilerParams(
            collective_id=0, has_side_effects=True, vmem_limit_bytes=12 * 2**20
        ),
        name="halo",
    )(kv)


def attention_kernel(
    cols_bound, rows_bound, ext_ref, q_ref, ga_ref, att_ref, dq_ref, dkv_ref,
    grads, k_turned, v_turned, bias, att_sum, dq_sum,
):
    row, col = place()
    row_first, col_first = row * 32, col * 16
    last_col = lax.axis_size("col") - 1
    exp_scale = DH ** (-0.5) * 1.4426950408889634

    for p in range(PAIRS):
        for cb in range(4):
            k_turned[p, cb] = ext_ref[cb, :, pl.ds(128 * p, SPAN)].T
            v_turned[p, cb] = ext_ref[cb, :, pl.ds(512 + 128 * p, SPAN)].T
    grads[...] = jnp.zeros_like(grads)
    att_sum[...] = jnp.zeros_like(att_sum)
    dq_sum[...] = jnp.zeros_like(dq_sum)

    at_row = lax.broadcasted_iota(jnp.int32, (SPAN, 128), 0)
    at_lane = lax.broadcasted_iota(jnp.int32, (128, SPAN), 1)

    def head_of(at, first):
        return (at >= first) & (at < first + DH)

    def split_turned(block, first):
        turned = block.T
        none = jnp.zeros_like(turned)
        return jnp.concatenate(
            [jnp.where(head_of(at_row, first + n * DH), turned, none) for n in range(2)], axis=1
        )

    def split_rows(block, first):
        none = jnp.zeros_like(block)
        return jnp.concatenate(
            [jnp.where(head_of(at_lane, first + n * DH), block, none) for n in range(2)], axis=0
        )

    def joined(turned, first):
        kept = jnp.where(
            head_of(at_row, first),
            turned[:, :128],
            jnp.where(head_of(at_row, first + DH), turned[:, 128:], 0.0),
        )
        return kept.T.reshape(16, 8, SPAN)

    def strip(s, _):
        j, t = s // 2, s % 2
        first_cb = jnp.where(col == 0, 1, jnp.where(col == last_col, 0, j))
        at = pl.multiple_of(128 * t, 128)
        band = pl.ds(at, 256)
        key_at = lax.broadcasted_iota(jnp.int32, (256, 128), 0)
        query_at = lax.broadcasted_iota(jnp.int32, (256, 128), 1)
        query_row = row_first + 16 * t + query_at // 8
        query_col = col_first + 8 * j + query_at % 8
        row_start = jnp.clip(query_row - REACH, 0, rows_bound)
        col_start = jnp.clip(query_col - REACH, 0, cols_bound)
        for b in range(3):
            key_row = row_first + 16 * t - REACH + key_at // 8
            key_col = col_first + 8 * (first_cb + b) - REACH + key_at % 8
            seen = (
                (key_row >= row_start)
                & (key_row <= row_start + 2 * REACH)
                & (key_col >= col_start)
                & (key_col <= col_start + 2 * REACH)
            )
            bias[b] = jnp.where(seen, 0.0, masked_score)
        for p in range(PAIRS):
            low, high = 16 * p, SHIFT + 16 * p
            here = pl.ds(128 * p, SPAN)
            there = pl.ds(512 + 128 * p, SPAN)
            query = q_ref[j, pl.ds(at, 128), here]
            upward = ga_ref[j, pl.ds(at, 128), here]
            query_turned = split_turned(query, low)
            upward_turned = split_turned(upward, high)
            scores = []
            for b in range(3):
                hidden = bias[b]
                scores.append(
                    mm(ext_ref[first_cb + b, band, here], query_turned)
                    + jnp.concatenate([hidden, hidden], axis=1)
                )
            top = functools.reduce(
                jnp.maximum, [jnp.max(x, axis=0, keepdims=True) for x in scores]
            )
            shifted = [jnp.exp2((x - top) * exp_scale) for x in scores]
            total = sum(jnp.sum(x, axis=0, keepdims=True) for x in shifted)
            inverse = 1.0 / total
            prob = [x * inverse for x in shifted]
            prob_low = [x.astype(bf16) for x in prob]
            dprob = [mm(ext_ref[first_cb + b, band, there], upward_turned) for b in range(3)]
            row_dot = sum(
                jnp.sum(x * y, axis=0, keepdims=True) for x, y in zip(prob, dprob)
            )
            dscore = [(x * (y - row_dot)).astype(bf16) for x, y in zip(prob, dprob)]
            att = sum(mm(v_turned[p, first_cb + b, :, band], prob_low[b]) for b in range(3))
            dquery = sum(mm(k_turned[p, first_cb + b, :, band], dscore[b]) for b in range(3))
            rows = pl.ds(16 * t, 16)
            att_sum[rows, j, :, here] += joined(att, high)
            dq_sum[rows, j, :, here] += joined(dquery, low)
            query_rows = split_rows(query, low)
            upward_rows = split_rows(upward, high)
            for b in range(3):
                grads[first_cb + b, band, here] += mm(dscore[b], query_rows)
                grads[first_cb + b, band, there] += mm(prob_low[b], upward_rows)
        return 0

    lax.fori_loop(0, 4, strip, 0)
    scale = DH ** (-0.5)
    att_ref[...] = att_sum[...].reshape(att_ref.shape).astype(bf16)
    dq_ref[...] = (dq_sum[...] * scale).reshape(dq_ref.shape).astype(bf16)
    for cb in range(4):
        dkv_ref[cb, :, :INNER] = (grads[cb, :, :INNER] * scale).astype(bf16)
        dkv_ref[cb, :, INNER:] = grads[cb, :, INNER:].astype(bf16)


def attention(ext, query, grad_att):
    rows = 32 * lax.axis_size("row")
    cols = 16 * lax.axis_size("col")
    tokens = 2 * query.shape[1]
    return pl.pallas_call(
        functools.partial(attention_kernel, cols - WINDOW, rows - WINDOW),
        out_shape=(
            jax.ShapeDtypeStruct((tokens, WIDE), bf16),
            jax.ShapeDtypeStruct((tokens, WIDE), bf16),
            jax.ShapeDtypeStruct(ext.shape, bf16),
        ),
        in_specs=[VMEM_SPEC] * 3,
        out_specs=(VMEM_SPEC,) * 3,
        scratch_shapes=[
            pltpu.VMEM(ext.shape, f32),
            pltpu.VMEM((PAIRS, 4, SPAN, 384), bf16),
            pltpu.VMEM((PAIRS, 4, SPAN, 384), bf16),
            pltpu.VMEM((3, 256, 128), f32),
            pltpu.VMEM((32, 2, 8, WIDE), f32),
            pltpu.VMEM((32, 2, 8, WIDE), f32),
        ],
        compiler_params=pltpu.CompilerParams(vmem_limit_bytes=36 * 2**20),
        name="attention",
    )(ext, query, grad_att)


PIECES = [(0, 64), (320, 64), (64, 256)]


def return_kernel(dkv_ref, out_ref, side, up_down, flat, total, send_col, recv_col, send_row, recv_row):
    row, col = place()
    greet_beside(row, col)

    def to_side(k, piece):
        first, size = PIECES[piece]
        return pltpu.make_async_remote_copy(
            src_ref=dkv_ref.at[3 * k, pl.ds(first, size)],
            dst_ref=side.at[k, pl.ds(first, size)],
            send_sem=send_col.at[k, piece],
            recv_sem=recv_col.at[k, piece],
            device_id={"row": row, "col": col + 2 * k - 1},
            device_id_type=MESH,
        )

    def to_row(k):
        return pltpu.make_async_remote_copy(
            src_ref=up_down.at[k],
            dst_ref=flat.at[k],
            send_sem=send_row.at[k],
            recv_sem=recv_row.at[k],
            device_id={"row": row + 2 * k - 1, "col": col},
            device_id_type=MESH,
        )

    def has_col(k):
        return inside(row, col + 2 * k - 1)

    def has_row(k):
        return inside(row + 2 * k - 1, col)

    for piece in range(3):
        for k in range(2):

            @pl.when(has_col(k))
            def _():
                to_side(k, piece).start()

    def gather(piece):
        first, size = PIECES[piece]
        at = pl.ds(first, size)
        total[:, at] = dkv_ref[1:3, at].astype(f32)
        for k in range(2):

            @pl.when(has_col(1 - k))
            def _():
                to_side(k, piece).wait_recv()
                total[1 - k, at] += side[k, at].astype(f32)

    for k in range(2):

        @pl.when(has_row(k))
        def _():
            gather(k)
            first, size = PIECES[k]
            up_down[k] = total[:, pl.ds(first, size)].astype(bf16)
            to_row(k).start()

        @pl.when(jnp.logical_not(has_row(k)))
        def _():
            for m in range(2):

                @pl.when(has_col(1 - m))
                def _():
                    to_side(m, k).wait_recv()

    gather(2)
    for k in range(2):

        @pl.when(has_row(1 - k))
        def _():
            to_row(k).wait_recv()
            first = 64 if k == 1 else 256
            total[:, pl.ds(first, 64)] += flat[k].astype(f32)

    mine = total[:, 64:320].reshape(2, 32, 8, 2 * INNER)
    out_ref[...] = jnp.stack([mine[0], mine[1]], axis=1).reshape(out_ref.shape).astype(bf16)

    for k in range(2):

        @pl.when(has_row(k))
        def _():
            to_row(k).wait_send()

        for piece in range(3):

            @pl.when(has_col(k))
            def _():
                to_side(k, piece).wait_send()


def returned(dkv):
    out = pl.pallas_call(
        return_kernel,
        out_shape=jax.ShapeDtypeStruct((512, 2 * INNER), bf16),
        in_specs=[VMEM_SPEC],
        out_specs=VMEM_SPEC,
        scratch_shapes=[
            pltpu.VMEM((2, 384, 2 * INNER), bf16),
            pltpu.VMEM((2, 2, 64, 2 * INNER), bf16),
            pltpu.VMEM((2, 2, 64, 2 * INNER), bf16),
            pltpu.VMEM((2, 384, 2 * INNER), f32),
            pltpu.SemaphoreType.DMA((2, 3)),
            pltpu.SemaphoreType.DMA((2, 3)),
            pltpu.SemaphoreType.DMA((2,)),
            pltpu.SemaphoreType.DMA((2,)),
        ],
        compiler_params=pltpu.CompilerParams(
            collective_id=1, has_side_effects=True, vmem_limit_bytes=24 * 2**20
        ),
        name="give_back",
    )(dkv)
    return out


def weight_kernel(tok_ref, up_ref, dq_ref, dkv_ref, att_ref, g_ref, turned):
    turned[0] = tok_ref[...].T
    turned[1] = up_ref[...].T

    def rows(n, _):
        at = pl.ds(pl.multiple_of(n * 288, 16), 288)
        for g in range(4):
            left = turned[1 if g == 3 else 0, at, :]
            right = (
                dq_ref[...],
                dkv_ref[:, :WIDE],
                dkv_ref[:, 2 * INNER - WIDE :],
                att_ref[...],
            )[g]
            g_ref[pl.ds(2 * n, 2), g] = mm(left, right).reshape(2, 144, WIDE).astype(bf16)
        return 0

    lax.fori_loop(0, 4, rows, 0)


def weight_grads(token_rows, grad_rows, dq, dkv, att):
    tokens, width = token_rows.shape
    return pl.pallas_call(
        weight_kernel,
        out_shape=jax.ShapeDtypeStruct((8, 4, 144, WIDE), bf16),
        in_specs=[VMEM_SPEC] * 5,
        out_specs=VMEM_SPEC,
        scratch_shapes=[pltpu.VMEM((2, width, tokens), bf16)],
        compiler_params=pltpu.CompilerParams(vmem_limit_bytes=24 * 2**20),
        name="weight_grads",
    )(token_rows, grad_rows, dq, dkv, att)


UPPER = 80


def sum_kernel(
    g_ref, dq_ref, dkv_ref, att_ref, wqkv_ref, wout_ref, out_ref, tokens_grad_ref, sublayer_ref, mine, recv0, rx1, ry1, a1, a2, rx2, ry2, b, rz, w, fin,
    sem0, sem_x1, sem_y1, sem_x2, sem_y2, send_z, recv_z, send_f, recv_f, local_sem,
):
    img = lax.axis_index("img")
    row, col = place()
    z_hi, y = row // 4, row % 4
    z_lo, core = col // 2, col % 2
    z = z_hi * 4 + z_lo
    other = 1 - core

    def device(img=img, z_hi=z_hi, y=y, z_lo=z_lo, core=core):
        return {"img": img, "row": z_hi * 4 + y, "col": z_lo * 2 + core}

    barrier = pltpu.get_barrier_semaphore()
    greeted = [device(core=other)]
    greeted += [device(img=(img + d) % 4) for d in range(1, 4)]
    greeted += [device(img=(img + d) % 4, core=other) for d in range(1, 4)]
    greeted += [device(y=(y + d) % 4) for d in range(1, 4)]
    for d in range(1, 8):
        z_there = (z + d) % 8
        greeted.append(device(z_hi=z_there // 4, z_lo=z_there % 4))
    for target in greeted:
        pl.semaphore_signal(barrier, inc=1, device_id=target, device_id_type=MESH)
    pl.semaphore_wait(barrier, len(greeted))

    def remote(src, dst, send, recv, target):
        return pltpu.make_async_remote_copy(
            src_ref=src, dst_ref=dst, send_sem=send, recv_sem=recv,
            device_id=target, device_id_type=MESH,
        )

    swaps, loads = [], []
    for k in range(4):
        swaps.append(
            remote(g_ref.at[other, k], recv0.at[k], sem0.at[0, k], sem0.at[1, k], device(core=other))
        )
        loads.append(pltpu.make_async_copy(g_ref.at[core, k], mine.at[k], local_sem.at[k]))
        swaps[k].start()
        loads[k].start()
    for k in range(4):
        loads[k].wait()
        swaps[k].wait_recv()

        def add(n, _):
            mine[k, n] = (mine[k, n].astype(f32) + recv0[k, n].astype(f32)).astype(bf16)
            return 0

        lax.fori_loop(0, 4, add, 0)

    first = []
    for d in range(1, 4):
        x_there, y_there = (img + d) % 4, (y + d) % 4
        first.append(
            remote(
                mine.at[:, x_there, :UPPER], rx1.at[d - 1],
                sem_x1.at[0, d - 1], sem_x1.at[1, d - 1], device(img=x_there),
            )
        )
        first.append(
            remote(
                mine.at[y_there, :, UPPER:], ry1.at[d - 1],
                sem_y1.at[0, d - 1], sem_y1.at[1, d - 1], device(y=y_there),
            )
        )
    for copy in first:
        copy.start()

    def products(n, _):
        at = pl.ds(pl.multiple_of(256 * n, 256), 256)
        tokens_grad = mm(dq_ref[at, :INNER], wqkv_ref[:INNER]) + mm(dkv_ref[at], wqkv_ref[INNER:])
        tokens_grad_ref[at] = tokens_grad.astype(bf16)
        sublayer_ref[at] = mm(att_ref[at, SHIFT:], wout_ref[...]).astype(bf16)
        return 0

    lax.fori_loop(0, 2, products, 0)
    for copy in first:
        copy.wait_recv()

    def add_first(n, _):
        upper = mine[n, img, :UPPER].astype(f32)
        lower = mine[y, n, UPPER:].astype(f32)
        for d in range(3):
            upper += rx1[d, n].astype(f32)
            lower += ry1[d, n].astype(f32)
        a1[n] = upper.astype(bf16)
        a2[n] = lower.astype(bf16)
        return 0

    lax.fori_loop(0, 4, add_first, 0)

    second = []
    for d in range(1, 4):
        x_there, y_there = (img + d) % 4, (y + d) % 4
        second.append(
            remote(
                a1.at[y_there], ry2.at[d - 1],
                sem_y2.at[0, d - 1], sem_y2.at[1, d - 1], device(y=y_there),
            )
        )
        second.append(
            remote(
                a2.at[x_there], rx2.at[d - 1],
                sem_x2.at[0, d - 1], sem_x2.at[1, d - 1], device(img=x_there),
            )
        )
    for copy in second:
        copy.start()
    for copy in second:
        copy.wait_recv()
    upper = a1[y].astype(f32)
    lower = a2[img].astype(f32)
    for d in range(3):
        upper += ry2[d].astype(f32)
        lower += rx2[d].astype(f32)
    b[:UPPER] = upper.astype(bf16)
    b[UPPER:] = lower.astype(bf16)

    holder = z_hi == core

    def to_chip(n):
        return remote(
            b.at[pl.ds(32 * n, 48)], rz.at[z], send_z.at[n], recv_z.at[z],
            device(z_hi=core, z_lo=n),
        )

    def from_chip(n):
        return remote(
            b.at[pl.ds(0, 48)], rz.at[n], send_z.at[0], recv_z.at[n], device(core=other)
        )

    for n in range(4):

        @pl.when(jnp.logical_not(holder & (z_lo == n)))
        def _():
            to_chip(n).start()

    def to_owner(d, k):
        return remote(
            w.at[pl.ds(16 * k, 32)], fin.at[img], send_f.at[d, k], recv_f.at[img],
            device(img=(img + d) % 4, core=k),
        )

    @pl.when(holder)
    def _():
        for n in range(8):

            @pl.when(z != n)
            def _():
                from_chip(n).wait_recv()

        own = b[pl.ds(pl.multiple_of(32 * z_lo, 32), 48)].astype(f32)
        rz[z] = own.astype(bf16)
        added = rz[0].astype(f32)
        for n in range(1, 8):
            added += rz[n].astype(f32)
        w[...] = added.astype(bf16)
        for d in range(4):
            for k in range(2):

                @pl.when((core != k) | (d != 0))
                def _():
                    to_owner(d, k).start()

        kept = pltpu.make_async_copy(
            w.at[pl.ds(pl.multiple_of(16 * core, 16), 32)], fin.at[img], local_sem.at[4]
        )
        kept.start()
        kept.wait()

    def from_holder(n):
        return remote(
            w.at[pl.ds(0, 32)], fin.at[n], send_f.at[0, 0], recv_f.at[n], device(core=other)
        )

    for n in range(4):

        @pl.when(jnp.logical_not(holder) | (img != n))
        def _():
            from_holder(n).wait_recv()

    out_ref[...] = fin[...]

    for copy in swaps + first + second:
        copy.wait_send()
    for n in range(4):

        @pl.when(jnp.logical_not(holder & (z_lo == n)))
        def _():
            to_chip(n).wait_send()

    @pl.when(holder)
    def _():
        for d in range(4):
            for k in range(2):

                @pl.when((core != k) | (d != 0))
                def _():
                    to_owner(d, k).wait_send()


def sum_over_devices(g, dq, dkv, att, qkv_turned, out_turned):
    rest = UPPER, 144 - UPPER
    dma = pltpu.SemaphoreType.DMA
    return pl.pallas_call(
        sum_kernel,
        out_shape=(
            jax.ShapeDtypeStruct((4, 32, WIDE), bf16),
            jax.ShapeDtypeStruct(dkv.shape, bf16),
            jax.ShapeDtypeStruct(dkv.shape, bf16),
        ),
        in_specs=[ANY_SPEC] + [VMEM_SPEC] * 5,
        out_specs=(VMEM_SPEC,) * 3,
        scratch_shapes=[
            pltpu.VMEM((4, 4, 144, WIDE), bf16),
            pltpu.VMEM((4, 4, 144, WIDE), bf16),
            pltpu.VMEM((3, 4, rest[0], WIDE), bf16),
            pltpu.VMEM((3, 4, rest[1], WIDE), bf16),
            pltpu.VMEM((4, rest[0], WIDE), bf16),
            pltpu.VMEM((4, rest[1], WIDE), bf16),
            pltpu.VMEM((3, rest[1], WIDE), bf16),
            pltpu.VMEM((3, rest[0], WIDE), bf16),
            pltpu.VMEM((144, WIDE), bf16),
            pltpu.VMEM((8, 48, WIDE), bf16),
            pltpu.VMEM((48, WIDE), bf16),
            pltpu.VMEM((4, 32, WIDE), bf16),
            dma((2, 4)),
            dma((2, 3)),
            dma((2, 3)),
            dma((2, 3)),
            dma((2, 3)),
            dma((4,)),
            dma((8,)),
            dma((4, 2)),
            dma((4,)),
            dma((5,)),
        ],
        compiler_params=pltpu.CompilerParams(
            collective_id=2, has_side_effects=True, vmem_limit_bytes=40 * 2**20
        ),
        name="sum_over_devices",
    )(g.reshape(2, 4, 4, 144, WIDE), dq, dkv, att, qkv_turned, out_turned)


def local(tokens, qkv_weight, out_weight, upstream):
    count = tokens.shape[1] * tokens.shape[2]
    width = tokens.shape[3]
    token_rows = tokens.reshape(count, width)
    grad_rows = upstream.reshape(count, width)
    query, keyvals, grad_att = project(token_rows, grad_rows, qkv_weight.T, out_weight.T)
    extended = with_halo(keyvals)
    att, dq, dkv = attention(extended, query, grad_att)
    dkv = returned(dkv)
    grads = weight_grads(token_rows, grad_rows, dq, dkv, att)
    shares, tokens_grad, sublayer_out = sum_over_devices(
        grads, dq, dkv, att, qkv_weight.T, out_weight.T
    )
    shares = lax.dynamic_slice_in_dim(shares, 2 * lax.axis_index("col"), 18, 1).astype(f32)
    qkv_grad = jnp.concatenate(
        [shares[0, :, :INNER], shares[1, :, :INNER], shares[2, :, SHIFT:]], axis=1
    )
    return (
        sublayer_out.reshape(tokens.shape),
        tokens_grad.reshape(tokens.shape),
        qkv_grad,
        shares[3, :, SHIFT:],
    )


def solution(mesh):
    return jax.shard_map(
        local,
        mesh=mesh,
        in_specs=(P("img", "row", "col", None), P(), P(), P("img", "row", "col", None)),
        out_specs=(
            P("img", "row", "col", None),
            P("img", "row", "col", None),
            P(("row", "col"), None),
            P(("row", "col"), None),
        ),
        check_vma=False,
    )
```

```python
import functools

import jax
import jax.numpy as jnp
from jax import lax
from jax.experimental import pallas as pl
from jax.experimental.pallas import tpu as pltpu
from jax.sharding import PartitionSpec as P

H = 8
DH = 72
REACH = 8
WINDOW = 17
INNER = H * DH
PAIRS = H // 2
SPAN = 256
WIDE = 640
SHIFT = 64

masked_score = -1e30
bf16 = jnp.bfloat16
f32 = jnp.float32
MESH = pl.DeviceIdType.MESH
VMEM_SPEC = pl.BlockSpec(memory_space=pltpu.VMEM)
HBM_SPEC = pl.BlockSpec(memory_space=pltpu.HBM)


def mm(a, b):
    return jnp.dot(a, b, preferred_element_type=f32)


def mm_nt(a, b):
    return lax.dot_general(a, b, (((1,), (1,)), ((), ())), preferred_element_type=f32)


def by_column_block(rows):
    count, width = rows.shape
    parts = rows.reshape(count // 16, 2, 8, width)
    return [parts[:, j].reshape(count // 2, width) for j in range(2)]


CORNERS = [(dr, dc) for dr in (-1, 1) for dc in (-1, 1)]


def halo_part(dr, dc):
    blocks = {-1: slice(0, 1), 0: slice(1, 3), 1: slice(3, 4)}[dc]
    tokens = {-1: slice(0, 64), 0: slice(64, 320), 1: slice(320, 384)}[dr]
    return blocks, tokens


def size_of(part):
    return tuple(s.stop - s.start for s in part)


def place():
    return lax.axis_index("row"), lax.axis_index("col")


def inside(row, col):
    rows, cols = lax.axis_size("row"), lax.axis_size("col")
    return (row >= 0) & (row < rows) & (col >= 0) & (col < cols)


def remote(src, dst, send, recv, target):
    return pltpu.make_async_remote_copy(
        src_ref=src, dst_ref=dst, send_sem=send, recv_sem=recv, device_id=target, device_id_type=MESH
    )


RELAYS = [(7, 0), (0, 1)]


def meets(row, col):
    ways = []
    for dr, dc in ((-1, 0), (1, 0), (0, -1), (0, 1)):
        across = ((row == 3) & (dr == 1)) | ((row == 4) & (dr == -1))
        ways.append((inside(row + dr, col + dc) & jnp.logical_not(across), row + dr, col + dc))
    at_relay = (row == 0) | (row == 7)
    at_edge = (row == 3) | (row == 4)
    for relay_row, edge_row in ((0, 3), (7, 4)):
        ways.append((at_relay | at_edge, jnp.where(at_relay, edge_row, relay_row), col))
    return ways


def greet(ways):
    barrier = pltpu.get_barrier_semaphore()
    count = jnp.int32(0)
    for there, row, col in ways:
        count = count + there.astype(jnp.int32)

        @pl.when(there)
        def _():
            pl.semaphore_signal(
                barrier, inc=1, device_id={"row": row, "col": col}, device_id_type=MESH
            )

    return barrier, count


class RowExchange:
    def __init__(self, row, col, src, dst, relay, send, recv, relay_send, relay_recv):
        self.row, self.col = row, col
        self.src, self.dst, self.relay = src, dst, relay
        self.send_sem, self.recv_sem = send, recv
        self.relay_send, self.relay_recv = relay_send, relay_recv

    def has(self, k):
        return inside(self.row + 2 * k - 1, self.col)

    def across(self, k):
        return self.row == (3 if k == 1 else 4)

    def direct(self, k, cb):
        target = {"row": self.row + 2 * k - 1, "col": self.col}
        return remote(
            self.src(k, cb), self.dst(k, cb), self.send_sem.at[k, cb], self.recv_sem.at[k, cb], target
        )

    def first(self, k, cb):
        target = {"row": RELAYS[cb][0], "col": self.col}
        return remote(
            self.src(k, cb), self.relay.at[k], self.send_sem.at[k, cb], self.relay_recv.at[k], target
        )

    def second(self, k, cb):
        target = {"row": 4 if k == 1 else 3, "col": self.col}
        return remote(
            self.relay.at[k], self.dst(k, cb), self.relay_send.at[k], self.recv_sem.at[k, cb], target
        )

    def start(self, k, cb):
        @pl.when(self.has(k) & jnp.logical_not(self.across(k)))
        def _():
            self.direct(k, cb).start()

        @pl.when(self.across(k))
        def _():
            self.first(k, cb).start()

    def pass_on(self):
        for relay_row, cb in RELAYS:

            @pl.when(self.row == relay_row)
            def _():
                for k in range(2):
                    self.first(k, cb).wait_recv()
                    self.second(k, cb).start()

    def wait_recv(self, k, cb):
        self.direct(k, cb).wait_recv()

    def wait_sends(self):
        for k in range(2):

            @pl.when(self.has(k))
            def _():
                for cb in range(2):
                    self.direct(k, cb).wait_send()

        for relay_row, cb in RELAYS:

            @pl.when(self.row == relay_row)
            def _():
                for k in range(2):
                    self.second(k, cb).wait_send()


def head_kernel(
    tok_hbm, up_hbm, wqkv_hbm, wout_hbm, q_ref, ga_ref, ext_ref, tok, up, wqkv, wout, relay,
    load_sem, send_row, recv_row, relay_send, relay_recv, send_col, recv_col,
):
    row, col = place()
    loads = [
        pltpu.make_async_copy(src, dst, load_sem.at[n])
        for n, (src, dst) in enumerate(
            (
                (tok_hbm, tok),
                (wqkv_hbm.at[pl.ds(INNER, 2 * INNER)], wqkv.at[pl.ds(INNER, 2 * INNER)]),
                (wqkv_hbm.at[pl.ds(0, INNER)], wqkv.at[pl.ds(0, INNER)]),
                (up_hbm, up),
                (wout_hbm, wout),
            )
        )
    ]
    for load in loads:
        load.start()
    barrier, count = greet(meets(row, col))
    loads[0].wait()
    loads[1].wait()
    x = tok[...]
    key = by_column_block(mm_nt(x, wqkv[INNER : 2 * INNER]))
    value = by_column_block(mm_nt(x, wqkv[2 * INNER :]))
    for j in range(2):
        ext_ref[1 + j, 64:320] = jnp.concatenate([key[j], value[j]], axis=1).astype(bf16)
    pl.semaphore_wait(barrier, count)

    rows = RowExchange(
        row, col,
        lambda k, cb: ext_ref.at[1 + cb, pl.ds(64 if k == 0 else 256, 64)],
        lambda k, cb: ext_ref.at[1 + cb, pl.ds(320 if k == 0 else 0, 64)],
        relay, send_row, recv_row, relay_send, relay_recv,
    )

    def sideways(n, dc):
        tokens = pl.ds((0, 320, 64)[n], (64, 64, 256)[n])
        k = (dc + 1) // 2
        return remote(
            ext_ref.at[2 if dc == -1 else 1, tokens], ext_ref.at[0 if dc == -1 else 3, tokens],
            send_col.at[k, n], recv_col.at[k, n], {"row": row, "col": col - dc},
        )

    for k in range(2):
        for cb in range(2):
            rows.start(k, cb)
    for dc in (-1, 1):

        @pl.when(inside(row, col - dc))
        def _():
            sideways(2, dc).start()

    for dr in (-1, 0, 1):
        for dc in (-1, 0, 1):
            if dr != 0 or dc != 0:

                @pl.when(jnp.logical_not(inside(row + dr, col + dc)))
                def _():
                    part = halo_part(dr, dc)
                    ext_ref[part] = jnp.zeros(size_of(part) + (2 * INNER,), bf16)

    loads[2].wait()
    query = by_column_block(mm_nt(x, wqkv[:WIDE]))
    for j in range(2):
        q_ref[j] = query[j].astype(bf16)
    loads[3].wait()
    loads[4].wait()
    grads = by_column_block(mm_nt(up[...], wout[...]))
    for j in range(2):
        blank = jnp.zeros((grads[j].shape[0], SHIFT), f32)
        ga_ref[j] = jnp.concatenate([blank, grads[j]], axis=1).astype(bf16)

    rows.pass_on()

    for n in range(2):
        for cb, dc in ((1, -1), (0, 1)):

            @pl.when(inside(row + 2 * n - 1, col))
            def _():
                rows.wait_recv(1 - n, cb)

            @pl.when(inside(row + 2 * n - 1, col) & inside(row, col - dc))
            def _():
                sideways(n, dc).start()

    for dc in (-1, 1):

        @pl.when(inside(row, col + dc))
        def _():
            sideways(2, dc).wait_recv()

        @pl.when(inside(row, col - dc))
        def _():
            sideways(2, dc).wait_send()

        for n in range(2):

            @pl.when(inside(row + 2 * n - 1, col + dc))
            def _():
                sideways(n, dc).wait_recv()

            @pl.when(inside(row + 2 * n - 1, col) & inside(row, col - dc))
            def _():
                sideways(n, dc).wait_send()

    rows.wait_sends()


def head(token_rows, grad_rows, qkv_turned, out_turned):
    dma = pltpu.SemaphoreType.DMA
    half = token_rows.shape[0] // 2
    return pl.pallas_call(
        head_kernel,
        out_shape=(
            jax.ShapeDtypeStruct((2, half, WIDE), bf16),
            jax.ShapeDtypeStruct((2, half, WIDE), bf16),
            jax.ShapeDtypeStruct((4, 384, 2 * INNER), bf16),
        ),
        in_specs=[HBM_SPEC] * 4,
        out_specs=(VMEM_SPEC,) * 3,
        scratch_shapes=[
            pltpu.VMEM(token_rows.shape, bf16),
            pltpu.VMEM(token_rows.shape, bf16),
            pltpu.VMEM(qkv_turned.shape, bf16),
            pltpu.VMEM(out_turned.shape, bf16),
            pltpu.VMEM((2, 64, 2 * INNER), bf16),
            dma((5,)),
            dma((2, 2)),
            dma((2, 2)),
            dma((2,)),
            dma((2,)),
            dma((2, 3)),
            dma((2, 3)),
        ],
        compiler_params=pltpu.CompilerParams(
            collective_id=0, has_side_effects=True, vmem_limit_bytes=32 * 2**20
        ),
        name="head",
    )(token_rows, grad_rows, qkv_turned, out_turned)


def attention_kernel(
    cols_bound, rows_bound, ext_ref, q_ref, ga_ref, att_ref, dq_ref, dkv_ref,
    grads, k_turned, v_turned, bias, att_sum, dq_sum,
):
    row, col = place()
    row_first, col_first = row * 32, col * 16
    last_col = lax.axis_size("col") - 1
    exp_scale = DH ** (-0.5) * 1.4426950408889634

    for p in range(PAIRS):
        for cb in range(4):
            k_turned[p, cb] = ext_ref[cb, :, pl.ds(128 * p, SPAN)].T
            v_turned[p, cb] = ext_ref[cb, :, pl.ds(512 + 128 * p, SPAN)].T
    grads[...] = jnp.zeros_like(grads)
    att_sum[...] = jnp.zeros_like(att_sum)
    dq_sum[...] = jnp.zeros_like(dq_sum)

    at_row = lax.broadcasted_iota(jnp.int32, (SPAN, 128), 0)
    at_lane = lax.broadcasted_iota(jnp.int32, (128, SPAN), 1)

    def head_of(at, first):
        return (at >= first) & (at < first + DH)

    def split_turned(block, first):
        turned = block.T
        none = jnp.zeros_like(turned)
        return jnp.concatenate(
            [jnp.where(head_of(at_row, first + n * DH), turned, none) for n in range(2)], axis=1
        )

    def split_rows(block, first):
        none = jnp.zeros_like(block)
        return jnp.concatenate(
            [jnp.where(head_of(at_lane, first + n * DH), block, none) for n in range(2)], axis=0
        )

    def joined(turned, first):
        kept = jnp.where(
            head_of(at_row, first),
            turned[:, :128],
            jnp.where(head_of(at_row, first + DH), turned[:, 128:], 0.0),
        )
        return kept.T.reshape(16, 8, SPAN)

    def strip(s, _):
        j, t = s // 2, s % 2
        first_cb = jnp.where(col == 0, 1, jnp.where(col == last_col, 0, j))
        at = pl.multiple_of(128 * t, 128)
        band = pl.ds(at, 256)
        key_at = lax.broadcasted_iota(jnp.int32, (256, 128), 0)
        query_at = lax.broadcasted_iota(jnp.int32, (256, 128), 1)
        query_row = row_first + 16 * t + query_at // 8
        query_col = col_first + 8 * j + query_at % 8
        row_start = jnp.clip(query_row - REACH, 0, rows_bound)
        col_start = jnp.clip(query_col - REACH, 0, cols_bound)
        for b in range(3):
            key_row = row_first + 16 * t - REACH + key_at // 8
            key_col = col_first + 8 * (first_cb + b) - REACH + key_at % 8
            seen = (
                (key_row >= row_start)
                & (key_row <= row_start + 2 * REACH)
                & (key_col >= col_start)
                & (key_col <= col_start + 2 * REACH)
            )
            bias[b] = jnp.where(seen, 0.0, masked_score)
        for p in range(PAIRS):
            low, high = 16 * p, SHIFT + 16 * p
            here = pl.ds(128 * p, SPAN)
            there = pl.ds(512 + 128 * p, SPAN)
            query = q_ref[j, pl.ds(at, 128), here]
            upward = ga_ref[j, pl.ds(at, 128), here]
            query_turned = split_turned(query, low)
            upward_turned = split_turned(upward, high)
            scores = []
            for b in range(3):
                hidden = bias[b]
                scores.append(
                    mm(ext_ref[first_cb + b, band, here], query_turned)
                    + jnp.concatenate([hidden, hidden], axis=1)
                )
            top = functools.reduce(
                jnp.maximum, [jnp.max(x, axis=0, keepdims=True) for x in scores]
            )
            shifted = [jnp.exp2((x - top) * exp_scale) for x in scores]
            total = sum(jnp.sum(x, axis=0, keepdims=True) for x in shifted)
            inverse = 1.0 / total
            prob = [x * inverse for x in shifted]
            prob_low = [x.astype(bf16) for x in prob]
            dprob = [mm(ext_ref[first_cb + b, band, there], upward_turned) for b in range(3)]
            row_dot = sum(
                jnp.sum(x * y, axis=0, keepdims=True) for x, y in zip(prob, dprob)
            )
            dscore = [(x * (y - row_dot)).astype(bf16) for x, y in zip(prob, dprob)]
            att = sum(mm(v_turned[p, first_cb + b, :, band], prob_low[b]) for b in range(3))
            dquery = sum(mm(k_turned[p, first_cb + b, :, band], dscore[b]) for b in range(3))
            rows = pl.ds(16 * t, 16)
            att_sum[rows, j, :, here] += joined(att, high)
            dq_sum[rows, j, :, here] += joined(dquery, low)
            query_rows = split_rows(query, low)
            upward_rows = split_rows(upward, high)
            for b in range(3):
                grads[first_cb + b, band, here] += mm(dscore[b], query_rows)
                grads[first_cb + b, band, there] += mm(prob_low[b], upward_rows)
        return 0

    lax.fori_loop(0, 4, strip, 0)
    scale = DH ** (-0.5)
    att_ref[...] = att_sum[...].reshape(att_ref.shape).astype(bf16)
    dq_ref[...] = (dq_sum[...] * scale).reshape(dq_ref.shape).astype(bf16)
    for cb in range(4):
        dkv_ref[cb, :, :INNER] = (grads[cb, :, :INNER] * scale).astype(bf16)
        dkv_ref[cb, :, INNER:] = grads[cb, :, INNER:].astype(bf16)


def attention(ext, query, grad_att):
    rows = 32 * lax.axis_size("row")
    cols = 16 * lax.axis_size("col")
    tokens = 2 * query.shape[1]
    return pl.pallas_call(
        functools.partial(attention_kernel, cols - WINDOW, rows - WINDOW),
        out_shape=(
            jax.ShapeDtypeStruct((tokens, WIDE), bf16),
            jax.ShapeDtypeStruct((tokens, WIDE), bf16),
            jax.ShapeDtypeStruct(ext.shape, bf16),
        ),
        in_specs=[VMEM_SPEC] * 3,
        out_specs=(VMEM_SPEC,) * 3,
        scratch_shapes=[
            pltpu.VMEM(ext.shape, f32),
            pltpu.VMEM((PAIRS, 4, SPAN, 384), bf16),
            pltpu.VMEM((PAIRS, 4, SPAN, 384), bf16),
            pltpu.VMEM((3, 256, 128), f32),
            pltpu.VMEM((32, 2, 8, WIDE), f32),
            pltpu.VMEM((32, 2, 8, WIDE), f32),
        ],
        compiler_params=pltpu.CompilerParams(vmem_limit_bytes=36 * 2**20),
        name="attention",
    )(ext, query, grad_att)


PIECES = [(0, 64), (320, 64), (64, 256)]
UPPER = 64
LOWER = 144 - UPPER
EARLY = (0, 3)


def tail_kernel(
    dkv_ref, dq_ref, att_ref, tok_ref, up_ref, wqkv_ref, wout_ref,
    out_ref, tokens_grad_ref, sublayer_ref,
    side, up_down, flat, relay, total, dkv_own, dkv_pair, pair, pair_rows, turned,
    mine, rx1, ry1, a1, a2, rx2, ry2, b, rz, w, fin,
    send_col, recv_col, send_row, recv_row, relay_send, relay_recv, pair_sem,
    sem_x1, sem_y1, sem_x2, sem_y2, send_z, recv_z, send_f, recv_f, local_sem,
):
    img = lax.axis_index("img")
    row, col = place()
    z_hi, y = row // 4, row % 4
    z_lo, core = col // 2, col % 2
    z = z_hi * 4 + z_lo
    other = 1 - core

    def device(img=img, z_hi=z_hi, y=y, z_lo=z_lo, core=core):
        return {"img": img, "row": z_hi * 4 + y, "col": z_lo * 2 + core}

    barrier, count = greet(meets(row, col))
    greeted = [device(core=other)]
    greeted += [device(img=(img + d) % 4) for d in range(1, 4)]
    greeted += [device(img=(img + d) % 4, core=other) for d in range(1, 4)]
    greeted += [device(y=(y + d) % 4) for d in range(1, 4)]
    for d in range(1, 8):
        z_there = (z + d) % 8
        greeted.append(device(z_hi=z_there // 4, z_lo=z_there % 4))
    for target in greeted:
        pl.semaphore_signal(barrier, inc=1, device_id=target, device_id_type=MESH)
    pl.semaphore_wait(barrier, count + len(greeted))

    def to_side(k, piece):
        at = pl.ds(*PIECES[piece])
        return remote(
            dkv_ref.at[3 * k, at], side.at[k, at], send_col.at[k, piece], recv_col.at[k, piece],
            {"row": row, "col": col + 2 * k - 1},
        )

    def has_col(k):
        return inside(row, col + 2 * k - 1)

    def has_row(k):
        return inside(row + 2 * k - 1, col)

    for piece in range(3):
        for k in range(2):

            @pl.when(has_col(k))
            def _():
                to_side(k, piece).start()

    def to_pair(n, src, dst):
        return remote(src, dst, pair_sem.at[0, n], pair_sem.at[1, n], device(core=other))

    lanes_there = pl.ds(pl.multiple_of(512 * other, 128), WIDE)
    lanes_here = pl.ds(pl.multiple_of(512 * core, 128), WIDE)
    swaps = [
        to_pair(0, up_ref.at[:, lanes_there], pair_rows.at[1]),
        to_pair(1, att_ref, pair.at[1]),
        to_pair(2, tok_ref.at[:, lanes_there], pair_rows.at[0]),
        to_pair(3, dq_ref, pair.at[0]),
    ]
    for swap in swaps:
        swap.start()
    turned[0, :, :512] = tok_ref[:, lanes_here].T
    turned[1, :, :512] = up_ref[:, lanes_here].T

    rows = RowExchange(
        row, col, lambda k, cb: up_down.at[k, cb], lambda k, cb: flat.at[k, cb],
        relay, send_row, recv_row, relay_send, relay_recv,
    )

    def gather(piece, cb):
        at = pl.ds(*PIECES[piece])
        total[cb, at] = dkv_ref[1 + cb, at].astype(f32)

        @pl.when(has_col(cb))
        def _():
            to_side(1 - cb, piece).wait_recv()
            total[cb, at] += side[1 - cb, at].astype(f32)

    for k in range(2):
        for cb in range(2):

            @pl.when(has_row(k))
            def _():
                gather(k, cb)
                up_down[k, cb] = total[cb, pl.ds(*PIECES[k])].astype(bf16)

            rows.start(k, cb)

            @pl.when(jnp.logical_not(has_row(k)) & has_col(cb))
            def _():
                to_side(1 - cb, k).wait_recv()

    def weight_part(group, own, theirs):
        which = 1 if group == 3 else 0

        def part(n, _):
            at = pl.ds(pl.multiple_of(64 * core + 288 * n, 16), 288)
            grad = mm(turned[which, at, :512], own()) + mm(turned[which, at, 512:], theirs())
            mine[pl.ds(2 * n, 2), group] = grad.reshape(2, 144, WIDE).astype(bf16)
            return 0

        lax.fori_loop(0, 2, part, 0)

    swaps[0].wait_recv()
    turned[1, :, 512:] = pair_rows[1].T
    swaps[1].wait_recv()
    weight_part(3, lambda: att_ref[...], lambda: pair[1])
    swaps[2].wait_recv()
    turned[0, :, 512:] = pair_rows[0].T
    swaps[3].wait_recv()
    weight_part(0, lambda: dq_ref[...], lambda: pair[0])
    rows.pass_on()

    def over_x(d):
        x_there = (img + d) % 4
        return remote(
            mine.at[:, x_there, :UPPER], rx1.at[d - 1],
            sem_x1.at[0, d - 1], sem_x1.at[1, d - 1], device(img=x_there),
        )

    def over_y(d, group):
        y_there = (y + d) % 4
        return remote(
            mine.at[y_there, group, UPPER:], ry1.at[d - 1, group],
            sem_y1.at[0, d - 1, group], sem_y1.at[1, d - 1, group], device(y=y_there),
        )

    def send_first(groups):
        for d in range(1, 4):
            x_there = (img + d) % 4

            @pl.when((x_there == groups[0]) | (x_there == groups[1]))
            def _():
                over_x(d).start()

            for group in groups:
                over_y(d, group).start()

    send_first(EARLY)

    def outward(n, _):
        at = pl.ds(pl.multiple_of(256 * n, 256), 256)
        sublayer_ref[at] = mm(att_ref[at, SHIFT:], wout_ref[...]).astype(bf16)
        return 0

    lax.fori_loop(0, 2, outward, 0)
    gather(2, 0)
    gather(2, 1)
    for k in range(2):

        @pl.when(has_row(1 - k))
        def _():
            first = 64 if k == 1 else 256
            for cb in range(2):
                rows.wait_recv(k, cb)
                total[cb, pl.ds(first, 64)] += flat[k, cb].astype(f32)

    owned = total[:, 64:320].reshape(2, 32, 8, 2 * INNER)
    dkv_own[...] = jnp.stack([owned[0], owned[1]], axis=1).reshape(dkv_own.shape).astype(bf16)
    swaps.append(to_pair(4, dkv_own, dkv_pair))
    swaps[4].start()
    swaps[4].wait_recv()
    weight_part(1, lambda: dkv_own[:, :WIDE], lambda: dkv_pair[:, :WIDE])
    weight_part(
        2, lambda: dkv_own[:, 2 * INNER - WIDE :], lambda: dkv_pair[:, 2 * INNER - WIDE :]
    )
    send_first((1, 2))

    def inward(n, _):
        at = pl.ds(pl.multiple_of(256 * n, 256), 256)
        grad = mm(dq_ref[at, :INNER], wqkv_ref[:INNER]) + mm(dkv_own[at], wqkv_ref[INNER:])
        tokens_grad_ref[at] = grad.astype(bf16)
        return 0

    lax.fori_loop(0, 2, inward, 0)
    for d in range(1, 4):
        over_x(d).wait_recv()
        for group in range(4):
            over_y(d, group).wait_recv()

    def add_first(n, _):
        upper = mine[n, img, :UPPER].astype(f32)
        lower = mine[y, n, UPPER:].astype(f32)
        for d in range(3):
            upper += rx1[d, n].astype(f32)
            lower += ry1[d, n].astype(f32)
        a1[n] = upper.astype(bf16)
        a2[n] = lower.astype(bf16)
        return 0

    lax.fori_loop(0, 4, add_first, 0)

    second = []
    for d in range(1, 4):
        x_there, y_there = (img + d) % 4, (y + d) % 4
        second.append(
            remote(
                a1.at[y_there], ry2.at[d - 1],
                sem_y2.at[0, d - 1], sem_y2.at[1, d - 1], device(y=y_there),
            )
        )
        second.append(
            remote(
                a2.at[x_there], rx2.at[d - 1],
                sem_x2.at[0, d - 1], sem_x2.at[1, d - 1], device(img=x_there),
            )
        )
    for copy in second:
        copy.start()
    for copy in second:
        copy.wait_recv()
    upper = a1[y].astype(f32)
    lower = a2[img].astype(f32)
    for d in range(3):
        upper += ry2[d].astype(f32)
        lower += rx2[d].astype(f32)
    b[:UPPER] = upper.astype(bf16)
    b[UPPER:] = lower.astype(bf16)

    holder = z_hi == core

    def to_chip(n):
        return remote(
            b.at[pl.ds(32 * n, 48)], rz.at[z], send_z.at[n], recv_z.at[z],
            device(z_hi=core, z_lo=n),
        )

    def from_chip(n):
        return remote(
            b.at[pl.ds(0, 48)], rz.at[n], send_z.at[0], recv_z.at[n], device(core=other)
        )

    for n in range(4):

        @pl.when(jnp.logical_not(holder & (z_lo == n)))
        def _():
            to_chip(n).start()

    def to_owner(d, k):
        return remote(
            w.at[pl.ds(16 * k, 32)], fin.at[img], send_f.at[d, k], recv_f.at[img],
            device(img=(img + d) % 4, core=k),
        )

    @pl.when(holder)
    def _():
        for n in range(8):

            @pl.when(z != n)
            def _():
                from_chip(n).wait_recv()

        own = b[pl.ds(pl.multiple_of(32 * z_lo, 32), 48)].astype(f32)
        rz[z] = own.astype(bf16)
        added = rz[0].astype(f32)
        for n in range(1, 8):
            added += rz[n].astype(f32)
        w[...] = added.astype(bf16)
        for d in range(4):
            for k in range(2):

                @pl.when((core != k) | (d != 0))
                def _():
                    to_owner(d, k).start()

        kept = pltpu.make_async_copy(
            w.at[pl.ds(pl.multiple_of(16 * core, 16), 32)], fin.at[img], local_sem.at[4]
        )
        kept.start()
        kept.wait()

    def from_holder(n):
        return remote(
            w.at[pl.ds(0, 32)], fin.at[n], send_f.at[0, 0], recv_f.at[n], device(core=other)
        )

    for n in range(4):

        @pl.when(jnp.logical_not(holder) | (img != n))
        def _():
            from_holder(n).wait_recv()

    out_ref[...] = fin[...]

    rows.wait_sends()
    for k in range(2):

        @pl.when(has_col(k))
        def _():
            for piece in range(3):
                to_side(k, piece).wait_send()

    for d in range(1, 4):
        over_x(d).wait_send()
        for group in range(4):
            over_y(d, group).wait_send()
    for copy in swaps + second:
        copy.wait_send()
    for n in range(4):

        @pl.when(jnp.logical_not(holder & (z_lo == n)))
        def _():
            to_chip(n).wait_send()

    @pl.when(holder)
    def _():
        for d in range(4):
            for k in range(2):

                @pl.when((core != k) | (d != 0))
                def _():
                    to_owner(d, k).wait_send()


def tail(dkv, dq, att, token_rows, grad_rows, qkv_turned, out_turned):
    dma = pltpu.SemaphoreType.DMA
    tokens, width = token_rows.shape
    return pl.pallas_call(
        tail_kernel,
        out_shape=(
            jax.ShapeDtypeStruct((4, 32, WIDE), bf16),
            jax.ShapeDtypeStruct(token_rows.shape, bf16),
            jax.ShapeDtypeStruct(token_rows.shape, bf16),
        ),
        in_specs=[VMEM_SPEC] * 7,
        out_specs=(VMEM_SPEC,) * 3,
        scratch_shapes=[
            pltpu.VMEM((2, 384, 2 * INNER), bf16),
            pltpu.VMEM((2, 2, 64, 2 * INNER), bf16),
            pltpu.VMEM((2, 2, 64, 2 * INNER), bf16),
            pltpu.VMEM((2, 64, 2 * INNER), bf16),
            pltpu.VMEM((2, 384, 2 * INNER), f32),
            pltpu.VMEM((tokens, 2 * INNER), bf16),
            pltpu.VMEM((tokens, 2 * INNER), bf16),
            pltpu.VMEM((2, tokens, WIDE), bf16),
            pltpu.VMEM((2, tokens, WIDE), bf16),
            pltpu.VMEM((2, WIDE, 2 * tokens), bf16),
            pltpu.VMEM((4, 4, 144, WIDE), bf16),
            pltpu.VMEM((3, 4, UPPER, WIDE), bf16),
            pltpu.VMEM((3, 4, LOWER, WIDE), bf16),
            pltpu.VMEM((4, UPPER, WIDE), bf16),
            pltpu.VMEM((4, LOWER, WIDE), bf16),
            pltpu.VMEM((3, LOWER, WIDE), bf16),
            pltpu.VMEM((3, UPPER, WIDE), bf16),
            pltpu.VMEM((144, WIDE), bf16),
            pltpu.VMEM((8, 48, WIDE), bf16),
            pltpu.VMEM((48, WIDE), bf16),
            pltpu.VMEM((4, 32, WIDE), bf16),
            dma((2, 3)),
            dma((2, 3)),
            dma((2, 2)),
            dma((2, 2)),
            dma((2,)),
            dma((2,)),
            dma((2, 5)),
            dma((2, 3)),
            dma((2, 3, 4)),
            dma((2, 3)),
            dma((2, 3)),
            dma((4,)),
            dma((8,)),
            dma((4, 2)),
            dma((4,)),
            dma((5,)),
        ],
        compiler_params=pltpu.CompilerParams(
            collective_id=1, has_side_effects=True, vmem_limit_bytes=48 * 2**20
        ),
        name="tail",
    )(dkv, dq, att, token_rows, grad_rows, qkv_turned, out_turned)


def local(tokens, qkv_weight, out_weight, upstream):
    count = tokens.shape[1] * tokens.shape[2]
    width = tokens.shape[3]
    token_rows = tokens.reshape(count, width)
    grad_rows = upstream.reshape(count, width)
    qkv_turned, out_turned = qkv_weight.T, out_weight.T
    query, grad_att, extended = head(token_rows, grad_rows, qkv_turned, out_turned)
    att, dq, dkv = attention(extended, query, grad_att)
    shares, tokens_grad, sublayer_out = tail(
        dkv, dq, att, token_rows, grad_rows, qkv_turned, out_turned
    )
    shares = lax.dynamic_slice_in_dim(shares, 2 * lax.axis_index("col"), 18, 1).astype(f32)
    qkv_grad = jnp.concatenate(
        [shares[0, :, :INNER], shares[1, :, :INNER], shares[2, :, SHIFT:]], axis=1
    )
    return (
        sublayer_out.reshape(tokens.shape),
        tokens_grad.reshape(tokens.shape),
        qkv_grad,
        shares[3, :, SHIFT:],
    )


def solution(mesh):
    return jax.shard_map(
        local,
        mesh=mesh,
        in_specs=(P("img", "row", "col", None), P(), P(), P("img", "row", "col", None)),
        out_specs=(
            P("img", "row", "col", None),
            P("img", "row", "col", None),
            P(("row", "col"), None),
            P(("row", "col"), None),
        ),
        check_vma=False,
    )
```

```python
import functools

import jax
import jax.numpy as jnp
from jax import lax
from jax.experimental import pallas as pl
from jax.experimental.pallas import tpu as pltpu
from jax.sharding import PartitionSpec as P

H = 8
DH = 72
REACH = 8
WINDOW = 17
INNER = H * DH
PAIRS = H // 2
SPAN = 256
WIDE = 640
SHIFT = 64

masked_score = -1e30
bf16 = jnp.bfloat16
f32 = jnp.float32
MESH = pl.DeviceIdType.MESH
VMEM_SPEC = pl.BlockSpec(memory_space=pltpu.VMEM)
ANY_SPEC = pl.BlockSpec(memory_space=pl.ANY)


def mm(a, b):
    return jnp.dot(a, b, preferred_element_type=f32)


def mm_nt(a, b):
    return lax.dot_general(a, b, (((1,), (1,)), ((), ())), preferred_element_type=f32)


def by_column_block(rows):
    count, width = rows.shape
    parts = rows.reshape(count // 16, 2, 8, width)
    return [parts[:, j].reshape(count // 2, width) for j in range(2)]


CORNERS = [(dr, dc) for dr in (-1, 1) for dc in (-1, 1)]


def halo_part(dr, dc):
    blocks = {-1: slice(0, 1), 0: slice(1, 3), 1: slice(3, 4)}[dc]
    tokens = {-1: slice(0, 64), 0: slice(64, 320), 1: slice(320, 384)}[dr]
    return blocks, tokens


def size_of(part):
    return tuple(s.stop - s.start for s in part)


def place():
    return lax.axis_index("row"), lax.axis_index("col")


def inside(row, col):
    rows, cols = lax.axis_size("row"), lax.axis_size("col")
    return (row >= 0) & (row < rows) & (col >= 0) & (col < cols)


def remote(src, dst, send, recv, target):
    return pltpu.make_async_remote_copy(
        src_ref=src, dst_ref=dst, send_sem=send, recv_sem=recv, device_id=target, device_id_type=MESH
    )


RELAYS = [(7, 0), (0, 1)]


def meets(row, col):
    ways = []
    for dr, dc in ((-1, 0), (1, 0), (0, -1), (0, 1)):
        across = ((row == 3) & (dr == 1)) | ((row == 4) & (dr == -1))
        ways.append((inside(row + dr, col + dc) & jnp.logical_not(across), row + dr, col + dc))
    at_relay = (row == 0) | (row == 7)
    at_edge = (row == 3) | (row == 4)
    for relay_row, edge_row in ((0, 3), (7, 4)):
        ways.append((at_relay | at_edge, jnp.where(at_relay, edge_row, relay_row), col))
    return ways


def greet(ways):
    barrier = pltpu.get_barrier_semaphore()
    count = jnp.int32(0)
    for there, row, col in ways:
        count = count + there.astype(jnp.int32)

        @pl.when(there)
        def _():
            pl.semaphore_signal(
                barrier, inc=1, device_id={"row": row, "col": col}, device_id_type=MESH
            )

    return barrier, count


class RowExchange:
    def __init__(self, row, col, src, dst, relay, send, recv, relay_send, relay_recv):
        self.row, self.col = row, col
        self.src, self.dst, self.relay = src, dst, relay
        self.send_sem, self.recv_sem = send, recv
        self.relay_send, self.relay_recv = relay_send, relay_recv

    def has(self, k):
        return inside(self.row + 2 * k - 1, self.col)

    def across(self, k):
        return self.row == (3 if k == 1 else 4)

    def direct(self, k, cb):
        target = {"row": self.row + 2 * k - 1, "col": self.col}
        return remote(
            self.src(k, cb), self.dst(k, cb), self.send_sem.at[k, cb], self.recv_sem.at[k, cb], target
        )

    def first(self, k, cb):
        target = {"row": RELAYS[cb][0], "col": self.col}
        return remote(
            self.src(k, cb), self.relay.at[k], self.send_sem.at[k, cb], self.relay_recv.at[k], target
        )

    def second(self, k, cb):
        target = {"row": 4 if k == 1 else 3, "col": self.col}
        return remote(
            self.relay.at[k], self.dst(k, cb), self.relay_send.at[k], self.recv_sem.at[k, cb], target
        )

    def start(self, k, cb):
        @pl.when(self.has(k) & jnp.logical_not(self.across(k)))
        def _():
            self.direct(k, cb).start()

        @pl.when(self.across(k))
        def _():
            self.first(k, cb).start()

    def pass_on(self):
        for relay_row, cb in RELAYS:

            @pl.when(self.row == relay_row)
            def _():
                for k in range(2):
                    self.first(k, cb).wait_recv()
                    self.second(k, cb).start()

    def wait_recv(self, k, cb):
        self.direct(k, cb).wait_recv()

    def wait_sends(self):
        for k in range(2):

            @pl.when(self.has(k))
            def _():
                for cb in range(2):
                    self.direct(k, cb).wait_send()

        for relay_row, cb in RELAYS:

            @pl.when(self.row == relay_row)
            def _():
                for k in range(2):
                    self.second(k, cb).wait_send()


def front_kernel(
    cols_bound, rows_bound, tok_hbm, up_hbm, wqkv_hbm, wout_hbm, ext_ref, att_ref, dq_ref, dkv_ref,
    tok, up, wqkv, wout, relay, kv_ext, query_all, upward_all, grads, k_turned, v_turned, bias, att_sum, dq_sum,
    load_sem, send_row, recv_row, relay_send, relay_recv, send_col, recv_col,
):
    row, col = place()
    loads = [
        pltpu.make_async_copy(src, dst, load_sem.at[n])
        for n, (src, dst) in enumerate(
            (
                (tok_hbm, tok),
                (wqkv_hbm.at[pl.ds(INNER, 2 * INNER)], wqkv.at[pl.ds(INNER, 2 * INNER)]),
                (wqkv_hbm.at[pl.ds(0, INNER)], wqkv.at[pl.ds(0, INNER)]),
                (up_hbm, up),
                (wout_hbm, wout),
            )
        )
    ]
    for load in loads:
        load.start()
    barrier, count = greet(meets(row, col))
    loads[0].wait()
    blocks = by_column_block(tok[...].astype(f32))
    for j in range(2):
        ext_ref[1 + j, 64:320] = blocks[j].astype(bf16)
    pl.semaphore_wait(barrier, count)

    rows = RowExchange(
        row, col,
        lambda k, cb: ext_ref.at[1 + cb, pl.ds(64 if k == 0 else 256, 64)],
        lambda k, cb: ext_ref.at[1 + cb, pl.ds(320 if k == 0 else 0, 64)],
        relay, send_row, recv_row, relay_send, relay_recv,
    )

    def sideways(n, dc):
        tokens = pl.ds((0, 320, 64)[n], (64, 64, 256)[n])
        k = (dc + 1) // 2
        return remote(
            ext_ref.at[2 if dc == -1 else 1, tokens], ext_ref.at[0 if dc == -1 else 3, tokens],
            send_col.at[k, n], recv_col.at[k, n], {"row": row, "col": col - dc},
        )

    for k in range(2):
        for cb in range(2):
            rows.start(k, cb)
    for dc in (-1, 1):

        @pl.when(inside(row, col - dc))
        def _():
            sideways(2, dc).start()

    for dr in (-1, 0, 1):
        for dc in (-1, 0, 1):
            if dr != 0 or dc != 0:

                @pl.when(jnp.logical_not(inside(row + dr, col + dc)))
                def _():
                    part = halo_part(dr, dc)
                    ext_ref[part] = jnp.zeros(size_of(part) + (2 * INNER,), bf16)

    grads[...] = jnp.zeros_like(grads)
    att_sum[...] = jnp.zeros_like(att_sum)
    dq_sum[...] = jnp.zeros_like(dq_sum)

    loads[1].wait()
    x = ext_ref[1:3, 64:320].reshape(512, 2 * INNER)
    keyvals = mm_nt(x, wqkv[INNER:])
    kv_ext[1:3, 64:320] = keyvals.astype(bf16).reshape(2, 256, 2 * INNER)
    loads[2].wait()
    query_all[...] = mm_nt(x, wqkv[:WIDE]).astype(bf16).reshape(query_all.shape)
    loads[3].wait()
    loads[4].wait()
    upward_grads = by_column_block(mm_nt(up[...], wout[...]))
    for j in range(2):
        blank = jnp.zeros((upward_grads[j].shape[0], SHIFT), f32)
        upward_all[j] = jnp.concatenate([blank, upward_grads[j]], axis=1).astype(bf16)

    def turn(chunk):
        lanes = pl.ds(128 * chunk, 128)
        for p in range(PAIRS):
            for cb in range(4):
                k_turned[p, cb, :, lanes] = kv_ext[cb, lanes, pl.ds(128 * p, SPAN)].T
                v_turned[p, cb, :, lanes] = kv_ext[cb, lanes, pl.ds(512 + 128 * p, SPAN)].T

    def pass_sideways(n):
        for cb, dc in ((1, -1), (0, 1)):

            @pl.when(inside(row + 2 * n - 1, col))
            def _():
                rows.wait_recv(1 - n, cb)

            @pl.when(inside(row + 2 * n - 1, col) & inside(row, col - dc))
            def _():
                sideways(n, dc).start()

    def finish_end(n):
        for dc in (-1, 1):

            @pl.when(inside(row + 2 * n - 1, col + dc))
            def _():
                sideways(n, dc).wait_recv()

        at = pl.ds((0, 320)[n], 64)
        ends = mm_nt(ext_ref[:, at].reshape(256, 2 * INNER), wqkv[INNER:])
        kv_ext[:, at] = ends.astype(bf16).reshape(4, 64, 2 * INNER)
        turn(2 * n)

    def near(n):
        return row != (4 if n == 0 else 3)

    rows.pass_on()
    for n in range(2):

        @pl.when(near(n))
        def _():
            pass_sideways(n)

    for dc in (-1, 1):

        @pl.when(inside(row, col + dc))
        def _():
            sideways(2, dc).wait_recv()

    x = jnp.concatenate([ext_ref[0, 64:320], ext_ref[3, 64:320]], axis=0)
    keyvals = mm_nt(x, wqkv[INNER:]).astype(bf16)
    kv_ext[0, 64:320] = keyvals[:256]
    kv_ext[3, 64:320] = keyvals[256:]
    turn(1)
    for n in range(2):

        @pl.when(near(n))
        def _():
            finish_end(n)

        @pl.when(jnp.logical_not(near(n)))
        def _():
            at = pl.ds((0, 320)[n], 64)
            kv_ext[:, at] = jnp.zeros((4, 64, 2 * INNER), bf16)

    row_first, col_first = row * 32, col * 16
    last_col = lax.axis_size("col") - 1
    exp_scale = DH ** (-0.5) * 1.4426950408889634

    at_row = lax.broadcasted_iota(jnp.int32, (SPAN, 128), 0)
    at_lane = lax.broadcasted_iota(jnp.int32, (128, SPAN), 1)

    def head_of(at, first):
        return (at >= first) & (at < first + DH)

    def split_turned(block, first):
        turned = block.T
        none = jnp.zeros_like(turned)
        return jnp.concatenate(
            [jnp.where(head_of(at_row, first + n * DH), turned, none) for n in range(2)], axis=1
        )

    def split_rows(block, first):
        none = jnp.zeros_like(block)
        return jnp.concatenate(
            [jnp.where(head_of(at_lane, first + n * DH), block, none) for n in range(2)], axis=0
        )

    def joined(turned, first):
        parts = [turned[:DH, :128], turned[DH:, 128:]]
        if first:
            parts = [jnp.zeros((first, 128), f32)] + parts
        if first + 2 * DH < SPAN:
            parts = parts + [jnp.zeros((SPAN - first - 2 * DH, 128), f32)]
        return jnp.concatenate(parts, axis=0).T.reshape(16, 8, SPAN)

    def strip(s, _):
        j = s % 2
        t = jnp.where(row == 4, 1 - s // 2, s // 2)
        for n, edge_row in ((1, 3), (0, 4)):

            @pl.when((s == 1) & (row == edge_row))
            def _():
                pass_sideways(n)

            @pl.when((s == 2) & (row == edge_row))
            def _():
                finish_end(n)

        first_cb = jnp.where(col == 0, 1, jnp.where(col == last_col, 0, j))
        at = pl.multiple_of(128 * t, 128)
        band = pl.ds(at, 256)
        key_at = lax.broadcasted_iota(jnp.int32, (256, 128), 0)
        query_at = lax.broadcasted_iota(jnp.int32, (256, 128), 1)
        query_row = row_first + 16 * t + query_at // 8
        query_col = col_first + 8 * j + query_at % 8
        row_start = jnp.clip(query_row - REACH, 0, rows_bound)
        col_start = jnp.clip(query_col - REACH, 0, cols_bound)
        for b in range(3):
            key_row = row_first + 16 * t - REACH + key_at // 8
            key_col = col_first + 8 * (first_cb + b) - REACH + key_at % 8
            seen = (
                (key_row >= row_start)
                & (key_row <= row_start + 2 * REACH)
                & (key_col >= col_start)
                & (key_col <= col_start + 2 * REACH)
            )
            bias[b] = jnp.where(seen, 0.0, masked_score)
        def weigh(p):
            low, high = 16 * p, SHIFT + 16 * p
            here = pl.ds(128 * p, SPAN)
            there = pl.ds(512 + 128 * p, SPAN)
            query_turned = split_turned(query_all[j, pl.ds(at, 128), here], low)
            upward_turned = split_turned(upward_all[j, pl.ds(at, 128), here], high)
            scores = []
            for b in range(3):
                hidden = bias[b]
                scores.append(
                    mm(kv_ext[first_cb + b, band, here], query_turned)
                    + jnp.concatenate([hidden, hidden], axis=1)
                )
            top = functools.reduce(
                jnp.maximum, [jnp.max(x, axis=0, keepdims=True) for x in scores]
            )
            shifted = [jnp.exp2((x - top) * exp_scale) for x in scores]
            total = sum(jnp.sum(x, axis=0, keepdims=True) for x in shifted)
            inverse = 1.0 / total
            prob = [x * inverse for x in shifted]
            prob_low = [x.astype(bf16) for x in prob]
            dprob = [mm(kv_ext[first_cb + b, band, there], upward_turned) for b in range(3)]
            row_dot = sum(
                jnp.sum(x * y, axis=0, keepdims=True) for x, y in zip(prob, dprob)
            )
            dscore = [(x * (y - row_dot)).astype(bf16) for x, y in zip(prob, dprob)]
            return prob_low, dscore

        def spread(p, prob_low, dscore):
            low, high = 16 * p, SHIFT + 16 * p
            here = pl.ds(128 * p, SPAN)
            there = pl.ds(512 + 128 * p, SPAN)
            att = sum(mm(v_turned[p, first_cb + b, high : high + 2 * DH, band], prob_low[b]) for b in range(3))
            dquery = sum(mm(k_turned[p, first_cb + b, low : low + 2 * DH, band], dscore[b]) for b in range(3))
            rows = pl.ds(16 * t, 16)
            att_sum[rows, j, :, here] += joined(att, high)
            dq_sum[rows, j, :, here] += joined(dquery, low)
            query_rows = split_rows(query_all[j, pl.ds(at, 128), here], low)
            upward_rows = split_rows(upward_all[j, pl.ds(at, 128), here], high)
            for b in range(3):
                grads[first_cb + b, band, here] += mm(dscore[b], query_rows)
                grads[first_cb + b, band, there] += mm(prob_low[b], upward_rows)

        ready = weigh(0)
        for p in range(PAIRS):
            later = weigh(p + 1) if p + 1 < PAIRS else None
            spread(p, *ready)
            ready = later
        return 0

    lax.fori_loop(0, 4, strip, 0)
    scale = DH ** (-0.5)
    att_ref[...] = att_sum[...].reshape(att_ref.shape).astype(bf16)
    dq_ref[...] = (dq_sum[...] * scale).reshape(dq_ref.shape).astype(bf16)
    for cb in range(4):
        dkv_ref[cb, :, :INNER] = (grads[cb, :, :INNER] * scale).astype(bf16)
        dkv_ref[cb, :, INNER:] = grads[cb, :, INNER:].astype(bf16)

    for dc in (-1, 1):

        @pl.when(inside(row, col - dc))
        def _():
            sideways(2, dc).wait_send()

        for n in range(2):

            @pl.when(inside(row + 2 * n - 1, col) & inside(row, col - dc))
            def _():
                sideways(n, dc).wait_send()

    rows.wait_sends()


def front(token_rows, grad_rows, qkv_turned, out_turned):
    dma = pltpu.SemaphoreType.DMA
    frame_rows = 32 * lax.axis_size("row")
    frame_cols = 16 * lax.axis_size("col")
    tokens, width = token_rows.shape
    extended = (4, 384, width)
    return pl.pallas_call(
        functools.partial(front_kernel, frame_cols - WINDOW, frame_rows - WINDOW),
        out_shape=(
            jax.ShapeDtypeStruct(extended, bf16),
            jax.ShapeDtypeStruct((tokens, WIDE), bf16),
            jax.ShapeDtypeStruct((tokens, WIDE), bf16),
            jax.ShapeDtypeStruct(extended, bf16),
        ),
        in_specs=[ANY_SPEC] * 4,
        out_specs=(VMEM_SPEC,) * 4,
        scratch_shapes=[
            pltpu.VMEM(token_rows.shape, bf16),
            pltpu.VMEM(token_rows.shape, bf16),
            pltpu.VMEM(qkv_turned.shape, bf16),
            pltpu.VMEM(out_turned.shape, bf16),
            pltpu.VMEM((2, 64, 2 * INNER), bf16),
            pltpu.VMEM(extended, bf16),
            pltpu.VMEM((2, 256, WIDE), bf16),
            pltpu.VMEM((2, 256, WIDE), bf16),
            pltpu.VMEM(extended, f32),
            pltpu.VMEM((PAIRS, 4, SPAN, 384), bf16),
            pltpu.VMEM((PAIRS, 4, SPAN, 384), bf16),
            pltpu.VMEM((3, 256, 128), f32),
            pltpu.VMEM((32, 2, 8, WIDE), f32),
            pltpu.VMEM((32, 2, 8, WIDE), f32),
            dma((5,)),
            dma((2, 2)),
            dma((2, 2)),
            dma((2,)),
            dma((2,)),
            dma((2, 3)),
            dma((2, 3)),
        ],
        compiler_params=pltpu.CompilerParams(
            collective_id=0, has_side_effects=True, vmem_limit_bytes=51 * 2**20
        ),
        name="front",
    )(token_rows, grad_rows, qkv_turned, out_turned)


PIECES = [(0, 64), (320, 64), (64, 256)]
UPPER = 80
LOWER = 144 - UPPER


def tail_kernel(
    ext_ref, dkv_ref, dq_ref, att_ref, tok_hbm, up_hbm, wqkv_hbm, wout_hbm,
    out_ref, tokens_grad_ref, sublayer_ref, tok_ref, up_ref, wqkv_ref, wout_ref,
    side, up_down, flat, relay, total, dkv_own, turned, ext_turned,
    mine, theirs, recv0, rx1, ry1, a1, a2, rx2, ry2, b, rz, w, fin,
    load_sem, send_col, recv_col, send_row, recv_row, relay_send, relay_recv, sem0,
    sem_x1, sem_y1, sem_x2, sem_y2, send_z, recv_z, send_f, recv_f, local_sem,
):
    img = lax.axis_index("img")
    row, col = place()
    z_hi, y = row // 4, row % 4
    z_lo, core = col // 2, col % 2
    z = z_hi * 4 + z_lo
    other = 1 - core

    def device(img=img, z_hi=z_hi, y=y, z_lo=z_lo, core=core):
        return {"img": img, "row": z_hi * 4 + y, "col": z_lo * 2 + core}

    loads = [
        pltpu.make_async_copy(src, dst, load_sem.at[n])
        for n, (src, dst) in enumerate(
            ((up_hbm, up_ref), (tok_hbm, tok_ref), (wout_hbm, wout_ref), (wqkv_hbm, wqkv_ref))
        )
    ]
    for load in loads:
        load.start()
    barrier, count = greet(meets(row, col))
    greeted = [device(core=other)]
    greeted += [device(img=(img + d) % 4) for d in range(1, 4)]
    greeted += [device(img=(img + d) % 4, core=other) for d in range(1, 4)]
    greeted += [device(y=(y + d) % 4) for d in range(1, 4)]
    for d in range(1, 8):
        z_there = (z + d) % 8
        greeted.append(device(z_hi=z_there // 4, z_lo=z_there % 4))
    for target in greeted:
        pl.semaphore_signal(barrier, inc=1, device_id=target, device_id_type=MESH)
    pl.semaphore_wait(barrier, count + len(greeted))

    def to_side(k, piece):
        at = pl.ds(*PIECES[piece])
        return remote(
            dkv_ref.at[3 * k, at], side.at[k, at], send_col.at[k, piece], recv_col.at[k, piece],
            {"row": row, "col": col + 2 * k - 1},
        )

    def has_col(k):
        return inside(row, col + 2 * k - 1)

    def has_row(k):
        return inside(row + 2 * k - 1, col)

    for piece in range(3):
        for k in range(2):

            @pl.when(has_col(k))
            def _():
                to_side(k, piece).start()

    rows = RowExchange(
        row, col, lambda k, cb: up_down.at[k, cb], lambda k, cb: flat.at[k, cb],
        relay, send_row, recv_row, relay_send, relay_recv,
    )

    def gather(piece, cb):
        at = pl.ds(*PIECES[piece])
        total[cb, at] = dkv_ref[1 + cb, at].astype(f32)

        @pl.when(has_col(cb))
        def _():
            to_side(1 - cb, piece).wait_recv()
            total[cb, at] += side[1 - cb, at].astype(f32)

    def return_ends():
        for k in range(2):
            for cb in range(2):

                @pl.when(has_row(k))
                def _():
                    gather(k, cb)
                    up_down[k, cb] = total[cb, pl.ds(*PIECES[k])].astype(bf16)

                rows.start(k, cb)

                @pl.when(jnp.logical_not(has_row(k)) & has_col(cb))
                def _():
                    to_side(1 - cb, k).wait_recv()

    def weight_rows(half, n, group):
        at = pl.ds(pl.multiple_of(576 * half + 288 * n, 32), 288)
        if group == 3:
            grad = mm(turned[1, at], att_ref[...])
        elif group == 0:
            grad = mm(turned[0, at], dq_ref[...])
        else:
            lanes = pl.ds(0 if group == 1 else 2 * INNER - WIDE, WIDE)
            grad = mm(ext_turned[at], dkv_ref[:, :, lanes].reshape(1536, WIDE))
        return grad.reshape(2, 144, WIDE)

    def swap(group):
        return remote(
            theirs.at[:, group], recv0.at[:, group], sem0.at[0, group], sem0.at[1, group],
            device(core=other),
        )

    def for_pair(group):
        def part(n, _):
            theirs[pl.ds(2 * n, 2), group] = weight_rows(other, n, group).astype(bf16)
            return 0

        lax.fori_loop(0, 2, part, 0)
        swap(group).start()

    def for_self(group):
        swap(group).wait_recv()

        def part(n, _):
            at = pl.ds(2 * n, 2)
            grad = weight_rows(core, n, group) + recv0[at, group].astype(f32)
            mine[at, group] = grad.astype(bf16)
            return 0

        lax.fori_loop(0, 2, part, 0)

    def over_x(d):
        x_there = (img + d) % 4
        return remote(
            mine.at[:, x_there, :UPPER], rx1.at[d - 1],
            sem_x1.at[0, d - 1], sem_x1.at[1, d - 1], device(img=x_there),
        )

    def over_y(d, group):
        y_there = (y + d) % 4
        return remote(
            mine.at[y_there, group, UPPER:], ry1.at[d - 1, group],
            sem_y1.at[0, d - 1, group], sem_y1.at[1, d - 1, group], device(y=y_there),
        )

    def send_first(group):
        for d in range(1, 4):

            @pl.when((img + d) % 4 == group)
            def _():
                over_x(d).start()

            over_y(d, group).start()

    loads[0].wait()
    turned[1] = up_ref[...].T
    for_pair(3)
    return_ends()
    loads[1].wait()
    turned[0] = tok_ref[...].T
    for_pair(0)
    for cb in range(4):
        ext_turned[:, pl.ds(384 * cb, 384)] = ext_ref[cb].T
    for_pair(1)
    for_self(3)
    send_first(3)
    for_pair(2)
    for_self(0)
    send_first(0)
    for_self(1)
    send_first(1)
    for_self(2)
    send_first(2)
    rows.pass_on()

    def outward(n, _):
        at = pl.ds(pl.multiple_of(256 * n, 256), 256)
        sublayer_ref[at] = mm(att_ref[at, SHIFT:], wout_ref[...]).astype(bf16)
        return 0

    loads[2].wait()
    lax.fori_loop(0, 2, outward, 0)
    gather(2, 0)
    gather(2, 1)
    for k in range(2):

        @pl.when(has_row(1 - k))
        def _():
            first = 64 if k == 1 else 256
            for cb in range(2):
                rows.wait_recv(k, cb)
                total[cb, pl.ds(first, 64)] += flat[k, cb].astype(f32)

    owned = total[:, 64:320].reshape(2, 32, 8, 2 * INNER)
    dkv_own[...] = jnp.stack([owned[0], owned[1]], axis=1).reshape(dkv_own.shape).astype(bf16)

    def inward(n, _):
        at = pl.ds(pl.multiple_of(256 * n, 256), 256)
        grad = mm(dq_ref[at, :INNER], wqkv_ref[:INNER]) + mm(dkv_own[at], wqkv_ref[INNER:])
        tokens_grad_ref[at] = grad.astype(bf16)
        return 0

    for d in range(1, 4):
        over_x(d).wait_recv()
        for group in range(4):
            over_y(d, group).wait_recv()

    def add_first(n, _):
        upper = mine[n, img, :UPPER].astype(f32)
        lower = mine[y, n, UPPER:].astype(f32)
        for d in range(3):
            upper += rx1[d, n].astype(f32)
            lower += ry1[d, n].astype(f32)
        a1[n] = upper.astype(bf16)
        a2[n] = lower.astype(bf16)
        return 0

    lax.fori_loop(0, 4, add_first, 0)

    second = []
    for d in range(1, 4):
        x_there, y_there = (img + d) % 4, (y + d) % 4
        second.append(
            remote(
                a1.at[y_there], ry2.at[d - 1],
                sem_y2.at[0, d - 1], sem_y2.at[1, d - 1], device(y=y_there),
            )
        )
        second.append(
            remote(
                a2.at[x_there], rx2.at[d - 1],
                sem_x2.at[0, d - 1], sem_x2.at[1, d - 1], device(img=x_there),
            )
        )
    for copy in second:
        copy.start()
    loads[3].wait()
    lax.fori_loop(0, 2, inward, 0)
    for copy in second:
        copy.wait_recv()
    upper = a1[y].astype(f32)
    lower = a2[img].astype(f32)
    for d in range(3):
        upper += ry2[d].astype(f32)
        lower += rx2[d].astype(f32)
    b[:UPPER] = upper.astype(bf16)
    b[UPPER:] = lower.astype(bf16)

    holder = z_hi == core

    def to_chip(n):
        return remote(
            b.at[pl.ds(32 * n, 48)], rz.at[z], send_z.at[n], recv_z.at[z],
            device(z_hi=core, z_lo=n),
        )

    def from_chip(n):
        return remote(
            b.at[pl.ds(0, 48)], rz.at[n], send_z.at[0], recv_z.at[n], device(core=other)
        )

    for n in range(4):

        @pl.when(jnp.logical_not(holder & (z_lo == n)))
        def _():
            to_chip(n).start()

    def to_owner(d, k):
        return remote(
            w.at[pl.ds(16 * k, 32)], fin.at[img], send_f.at[d, k], recv_f.at[img],
            device(img=(img + d) % 4, core=k),
        )

    @pl.when(holder)
    def _():
        for n in range(8):

            @pl.when(z != n)
            def _():
                from_chip(n).wait_recv()

        own = b[pl.ds(pl.multiple_of(32 * z_lo, 32), 48)].astype(f32)
        rz[z] = own.astype(bf16)
        added = rz[0].astype(f32)
        for n in range(1, 8):
            added += rz[n].astype(f32)
        w[...] = added.astype(bf16)
        for d in range(4):
            for k in range(2):

                @pl.when((core != k) | (d != 0))
                def _():
                    to_owner(d, k).start()

        kept = pltpu.make_async_copy(
            w.at[pl.ds(pl.multiple_of(16 * core, 16), 32)], fin.at[img], local_sem.at[4]
        )
        kept.start()
        kept.wait()

    def from_holder(n):
        return remote(
            w.at[pl.ds(0, 32)], fin.at[n], send_f.at[0, 0], recv_f.at[n], device(core=other)
        )

    for n in range(4):

        @pl.when(jnp.logical_not(holder) | (img != n))
        def _():
            from_holder(n).wait_recv()

    out_ref[...] = fin[...]

    rows.wait_sends()
    for k in range(2):

        @pl.when(has_col(k))
        def _():
            for piece in range(3):
                to_side(k, piece).wait_send()

    for d in range(1, 4):
        over_x(d).wait_send()
        for group in range(4):
            over_y(d, group).wait_send()
    for group in range(4):
        swap(group).wait_send()
    for copy in second:
        copy.wait_send()
    for n in range(4):

        @pl.when(jnp.logical_not(holder & (z_lo == n)))
        def _():
            to_chip(n).wait_send()

    @pl.when(holder)
    def _():
        for d in range(4):
            for k in range(2):

                @pl.when((core != k) | (d != 0))
                def _():
                    to_owner(d, k).wait_send()


def tail(ext, dkv, dq, att, token_rows, grad_rows, qkv_turned, out_turned):
    dma = pltpu.SemaphoreType.DMA
    tokens, width = token_rows.shape
    return pl.pallas_call(
        tail_kernel,
        out_shape=(
            jax.ShapeDtypeStruct((4, 32, WIDE), bf16),
            jax.ShapeDtypeStruct(token_rows.shape, bf16),
            jax.ShapeDtypeStruct(token_rows.shape, bf16),
        ),
        in_specs=[VMEM_SPEC] * 4 + [ANY_SPEC] * 4,
        out_specs=(VMEM_SPEC,) * 3,
        scratch_shapes=[
            pltpu.VMEM(token_rows.shape, bf16),
            pltpu.VMEM(token_rows.shape, bf16),
            pltpu.VMEM(qkv_turned.shape, bf16),
            pltpu.VMEM(out_turned.shape, bf16),
            pltpu.VMEM((2, 384, 2 * INNER), bf16),
            pltpu.VMEM((2, 2, 64, 2 * INNER), bf16),
            pltpu.VMEM((2, 2, 64, 2 * INNER), bf16),
            pltpu.VMEM((2, 64, 2 * INNER), bf16),
            pltpu.VMEM((2, 384, 2 * INNER), f32),
            pltpu.VMEM((tokens, 2 * INNER), bf16),
            pltpu.VMEM((2, width, tokens), bf16),
            pltpu.VMEM((width, 4 * 384), bf16),
            pltpu.VMEM((4, 4, 144, WIDE), bf16),
            pltpu.VMEM((4, 4, 144, WIDE), bf16),
            pltpu.VMEM((4, 4, 144, WIDE), bf16),
            pltpu.VMEM((3, 4, UPPER, WIDE), bf16),
            pltpu.VMEM((3, 4, LOWER, WIDE), bf16),
            pltpu.VMEM((4, UPPER, WIDE), bf16),
            pltpu.VMEM((4, LOWER, WIDE), bf16),
            pltpu.VMEM((3, LOWER, WIDE), bf16),
            pltpu.VMEM((3, UPPER, WIDE), bf16),
            pltpu.VMEM((144, WIDE), bf16),
            pltpu.VMEM((8, 48, WIDE), bf16),
            pltpu.VMEM((48, WIDE), bf16),
            pltpu.VMEM((4, 32, WIDE), bf16),
            dma((4,)),
            dma((2, 3)),
            dma((2, 3)),
            dma((2, 2)),
            dma((2, 2)),
            dma((2,)),
            dma((2,)),
            dma((2, 4)),
            dma((2, 3)),
            dma((2, 3, 4)),
            dma((2, 3)),
            dma((2, 3)),
            dma((4,)),
            dma((8,)),
            dma((4, 2)),
            dma((4,)),
            dma((5,)),
        ],
        compiler_params=pltpu.CompilerParams(
            collective_id=1, has_side_effects=True, vmem_limit_bytes=50 * 2**20
        ),
        name="tail",
    )(ext, dkv, dq, att, token_rows, grad_rows, qkv_turned, out_turned)


def local(tokens, qkv_weight, out_weight, upstream):
    count = tokens.shape[1] * tokens.shape[2]
    width = tokens.shape[3]
    token_rows = tokens.reshape(count, width)
    grad_rows = upstream.reshape(count, width)
    qkv_turned, out_turned = qkv_weight.T, out_weight.T
    extended, att, dq, dkv = front(token_rows, grad_rows, qkv_turned, out_turned)
    shares, tokens_grad, sublayer_out = tail(
        extended, dkv, dq, att, token_rows, grad_rows, qkv_turned, out_turned
    )
    shares = lax.dynamic_slice_in_dim(shares, 2 * lax.axis_index("col"), 18, 1).astype(f32)
    qkv_grad = jnp.concatenate(
        [shares[0, :, :INNER], shares[1, :, :INNER], shares[2, :, SHIFT:]], axis=1
    )
    return (
        sublayer_out.reshape(tokens.shape),
        tokens_grad.reshape(tokens.shape),
        qkv_grad,
        shares[3, :, SHIFT:],
    )


def solution(mesh):
    return jax.shard_map(
        local,
        mesh=mesh,
        in_specs=(P("img", "row", "col", None), P(), P(), P("img", "row", "col", None)),
        out_specs=(
            P("img", "row", "col", None),
            P("img", "row", "col", None),
            P(("row", "col"), None),
            P(("row", "col"), None),
        ),
        check_vma=False,
    )
```

```python
import functools

import jax
import jax.numpy as jnp
from jax import lax
from jax.experimental import pallas as pl
from jax.experimental.pallas import tpu as pltpu
from jax.sharding import PartitionSpec as P

H = 8
DH = 72
REACH = 8
WINDOW = 17
INNER = H * DH
PAIRS = H // 2
SPAN = 256
WIDE = 640
SHIFT = 64

masked_score = -1e30
bf16 = jnp.bfloat16
f32 = jnp.float32
MESH = pl.DeviceIdType.MESH
VMEM_SPEC = pl.BlockSpec(memory_space=pltpu.VMEM)
ANY_SPEC = pl.BlockSpec(memory_space=pl.ANY)


def mm(a, b):
    return jnp.dot(a, b, preferred_element_type=f32)


def mm_nt(a, b):
    return lax.dot_general(a, b, (((1,), (1,)), ((), ())), preferred_element_type=f32)


def by_column_block(rows):
    count, width = rows.shape
    parts = rows.reshape(count // 16, 2, 8, width)
    return [parts[:, j].reshape(count // 2, width) for j in range(2)]


CORNERS = [(dr, dc) for dr in (-1, 1) for dc in (-1, 1)]


def halo_part(dr, dc):
    blocks = {-1: slice(0, 1), 0: slice(1, 3), 1: slice(3, 4)}[dc]
    tokens = {-1: slice(0, 64), 0: slice(64, 320), 1: slice(320, 384)}[dr]
    return blocks, tokens


def size_of(part):
    return tuple(s.stop - s.start for s in part)


def place():
    return lax.axis_index("row"), lax.axis_index("col")


def inside(row, col):
    rows, cols = lax.axis_size("row"), lax.axis_size("col")
    return (row >= 0) & (row < rows) & (col >= 0) & (col < cols)


def remote(src, dst, send, recv, target):
    return pltpu.make_async_remote_copy(
        src_ref=src, dst_ref=dst, send_sem=send, recv_sem=recv, device_id=target, device_id_type=MESH
    )


RELAYS = [(7, 0), (0, 1)]


def meets(row, col):
    ways = []
    for dr, dc in ((-1, 0), (1, 0), (0, -1), (0, 1)):
        across = ((row == 3) & (dr == 1)) | ((row == 4) & (dr == -1))
        ways.append((inside(row + dr, col + dc) & jnp.logical_not(across), row + dr, col + dc))
    at_relay = (row == 0) | (row == 7)
    at_edge = (row == 3) | (row == 4)
    for relay_row, edge_row in ((0, 3), (7, 4)):
        ways.append((at_relay | at_edge, jnp.where(at_relay, edge_row, relay_row), col))
    return ways


def greet(ways):
    barrier = pltpu.get_barrier_semaphore()
    count = jnp.int32(0)
    for there, row, col in ways:
        count = count + there.astype(jnp.int32)

        @pl.when(there)
        def _():
            pl.semaphore_signal(
                barrier, inc=1, device_id={"row": row, "col": col}, device_id_type=MESH
            )

    return barrier, count


class RowExchange:
    def __init__(self, row, col, src, dst, relay, send, recv, relay_send, relay_recv):
        self.row, self.col = row, col
        self.src, self.dst, self.relay = src, dst, relay
        self.send_sem, self.recv_sem = send, recv
        self.relay_send, self.relay_recv = relay_send, relay_recv

    def has(self, k):
        return inside(self.row + 2 * k - 1, self.col)

    def across(self, k):
        return self.row == (3 if k == 1 else 4)

    def direct(self, k, cb):
        target = {"row": self.row + 2 * k - 1, "col": self.col}
        return remote(
            self.src(k, cb), self.dst(k, cb), self.send_sem.at[k, cb], self.recv_sem.at[k, cb], target
        )

    def first(self, k, cb):
        target = {"row": RELAYS[cb][0], "col": self.col}
        return remote(
            self.src(k, cb), self.relay.at[k], self.send_sem.at[k, cb], self.relay_recv.at[k], target
        )

    def second(self, k, cb):
        target = {"row": 4 if k == 1 else 3, "col": self.col}
        return remote(
            self.relay.at[k], self.dst(k, cb), self.relay_send.at[k], self.recv_sem.at[k, cb], target
        )

    def start(self, k, cb):
        @pl.when(self.has(k) & jnp.logical_not(self.across(k)))
        def _():
            self.direct(k, cb).start()

        @pl.when(self.across(k))
        def _():
            self.first(k, cb).start()

    def pass_on(self, late):
        for relay_row, cb in RELAYS:
            k = 1 - cb if late else cb

            @pl.when(self.row == relay_row)
            def _():
                self.first(k, cb).wait_recv()
                self.second(k, cb).start()

    def wait_recv(self, k, cb):
        self.direct(k, cb).wait_recv()

    def wait_sends(self):
        for k in range(2):

            @pl.when(self.has(k))
            def _():
                for cb in range(2):
                    self.direct(k, cb).wait_send()

        for relay_row, cb in RELAYS:

            @pl.when(self.row == relay_row)
            def _():
                for k in range(2):
                    self.second(k, cb).wait_send()


def front_kernel(
    cols_bound, rows_bound, tok_hbm, up_hbm, wqkv_hbm, wout_hbm, ext_ref, att_ref, dq_ref, dkv_ref,
    tok, up, wqkv, wout, relay, kv_ext, query_all, upward_all, grads, k_turned, v_turned, bias, att_sum, dq_sum,
    load_sem, send_row, recv_row, relay_send, relay_recv, send_col, recv_col,
):
    row, col = place()
    loads = [
        pltpu.make_async_copy(src, dst, load_sem.at[n])
        for n, (src, dst) in enumerate(
            (
                (tok_hbm, tok),
                (wqkv_hbm.at[pl.ds(INNER, 2 * INNER)], wqkv.at[pl.ds(INNER, 2 * INNER)]),
                (wqkv_hbm.at[pl.ds(0, INNER)], wqkv.at[pl.ds(0, INNER)]),
                (up_hbm, up),
                (wout_hbm, wout),
            )
        )
    ]
    for load in loads:
        load.start()
    barrier, count = greet(meets(row, col))
    loads[0].wait()
    blocks = by_column_block(tok[...].astype(f32))
    for j in range(2):
        ext_ref[1 + j, 64:320] = blocks[j].astype(bf16)
    pl.semaphore_wait(barrier, count)

    rows = RowExchange(
        row, col,
        lambda k, cb: ext_ref.at[1 + cb, pl.ds(64 if k == 0 else 256, 64)],
        lambda k, cb: ext_ref.at[1 + cb, pl.ds(320 if k == 0 else 0, 64)],
        relay, send_row, recv_row, relay_send, relay_recv,
    )

    def sideways(n, dc):
        tokens = pl.ds((0, 320, 64)[n], (64, 64, 256)[n])
        k = (dc + 1) // 2
        return remote(
            ext_ref.at[2 if dc == -1 else 1, tokens], ext_ref.at[0 if dc == -1 else 3, tokens],
            send_col.at[k, n], recv_col.at[k, n], {"row": row, "col": col - dc},
        )

    for k in range(2):
        for cb in range(2):
            rows.start(k, cb)
    for dc in (-1, 1):

        @pl.when(inside(row, col - dc))
        def _():
            sideways(2, dc).start()

    for dr in (-1, 0, 1):
        for dc in (-1, 0, 1):
            if dr != 0 or dc != 0:

                @pl.when(jnp.logical_not(inside(row + dr, col + dc)))
                def _():
                    part = halo_part(dr, dc)
                    ext_ref[part] = jnp.zeros(size_of(part) + (2 * INNER,), bf16)

    grads[...] = jnp.zeros_like(grads)
    att_sum[...] = jnp.zeros_like(att_sum)
    dq_sum[...] = jnp.zeros_like(dq_sum)

    loads[1].wait()
    x = ext_ref[1:3, 64:320].reshape(512, 2 * INNER)
    keyvals = mm_nt(x, wqkv[INNER:])
    kv_ext[1:3, 64:320] = keyvals.astype(bf16).reshape(2, 256, 2 * INNER)
    loads[2].wait()
    query_all[...] = mm_nt(x, wqkv[:WIDE]).astype(bf16).reshape(query_all.shape)
    loads[3].wait()
    loads[4].wait()
    upward_grads = by_column_block(mm_nt(up[...], wout[...]))
    for j in range(2):
        blank = jnp.zeros((upward_grads[j].shape[0], SHIFT), f32)
        upward_all[j] = jnp.concatenate([blank, upward_grads[j]], axis=1).astype(bf16)

    def turn(chunk):
        lanes = pl.ds(128 * chunk, 128)
        for p in range(PAIRS):
            for cb in range(4):
                k_turned[p, cb, :, lanes] = kv_ext[cb, lanes, pl.ds(128 * p, SPAN)].T
                v_turned[p, cb, :, lanes] = kv_ext[cb, lanes, pl.ds(512 + 128 * p, SPAN)].T

    def pass_sideways(n):
        for cb, dc in ((1, -1), (0, 1)):

            @pl.when(inside(row + 2 * n - 1, col))
            def _():
                rows.wait_recv(1 - n, cb)

            @pl.when(inside(row + 2 * n - 1, col) & inside(row, col - dc))
            def _():
                sideways(n, dc).start()

    def finish_end(n):
        for dc in (-1, 1):

            @pl.when(inside(row + 2 * n - 1, col + dc))
            def _():
                sideways(n, dc).wait_recv()

        at = pl.ds((0, 320)[n], 64)
        ends = mm_nt(ext_ref[:, at].reshape(256, 2 * INNER), wqkv[INNER:])
        kv_ext[:, at] = ends.astype(bf16).reshape(4, 64, 2 * INNER)
        turn(2 * n)

    def near(n):
        return row != (4 if n == 0 else 3)

    rows.pass_on(False)
    for n in range(2):

        @pl.when(near(n))
        def _():
            pass_sideways(n)

    for dc in (-1, 1):

        @pl.when(inside(row, col + dc))
        def _():
            sideways(2, dc).wait_recv()

    x = jnp.concatenate([ext_ref[0, 64:320], ext_ref[3, 64:320]], axis=0)
    keyvals = mm_nt(x, wqkv[INNER:]).astype(bf16)
    kv_ext[0, 64:320] = keyvals[:256]
    kv_ext[3, 64:320] = keyvals[256:]
    turn(1)
    for n in range(2):

        @pl.when(near(n))
        def _():
            finish_end(n)

        @pl.when(jnp.logical_not(near(n)))
        def _():
            at = pl.ds((0, 320)[n], 64)
            kv_ext[:, at] = jnp.zeros((4, 64, 2 * INNER), bf16)

    rows.pass_on(True)
    row_first, col_first = row * 32, col * 16
    last_col = lax.axis_size("col") - 1
    exp_scale = DH ** (-0.5) * 1.4426950408889634

    at_row = lax.broadcasted_iota(jnp.int32, (SPAN, 128), 0)
    at_lane = lax.broadcasted_iota(jnp.int32, (128, SPAN), 1)

    def head_of(at, first):
        return (at >= first) & (at < first + DH)

    def split_turned(block, first):
        turned = block.T
        none = jnp.zeros_like(turned)
        return jnp.concatenate(
            [jnp.where(head_of(at_row, first + n * DH), turned, none) for n in range(2)], axis=1
        )

    def split_rows(block, first):
        none = jnp.zeros_like(block)
        return jnp.concatenate(
            [jnp.where(head_of(at_lane, first + n * DH), block, none) for n in range(2)], axis=0
        )

    def joined(turned, first):
        parts = [turned[:DH, :128], turned[DH:, 128:]]
        if first:
            parts = [jnp.zeros((first, 128), f32)] + parts
        if first + 2 * DH < SPAN:
            parts = parts + [jnp.zeros((SPAN - first - 2 * DH, 128), f32)]
        return jnp.concatenate(parts, axis=0).T.reshape(16, 8, SPAN)

    def strip(s, _):
        j = s % 2
        t = jnp.where(row == 4, 1 - s // 2, s // 2)
        for n, edge_row in ((1, 3), (0, 4)):

            @pl.when((s == 1) & (row == edge_row))
            def _():
                pass_sideways(n)

            @pl.when((s == 2) & (row == edge_row))
            def _():
                finish_end(n)

        first_cb = jnp.where(col == 0, 1, jnp.where(col == last_col, 0, j))
        at = pl.multiple_of(128 * t, 128)
        band = pl.ds(at, 256)
        key_at = lax.broadcasted_iota(jnp.int32, (256, 128), 0)
        query_at = lax.broadcasted_iota(jnp.int32, (256, 128), 1)
        query_row = row_first + 16 * t + query_at // 8
        query_col = col_first + 8 * j + query_at % 8
        row_start = jnp.clip(query_row - REACH, 0, rows_bound)
        col_start = jnp.clip(query_col - REACH, 0, cols_bound)
        for b in range(3):
            key_row = row_first + 16 * t - REACH + key_at // 8
            key_col = col_first + 8 * (first_cb + b) - REACH + key_at % 8
            seen = (
                (key_row >= row_start)
                & (key_row <= row_start + 2 * REACH)
                & (key_col >= col_start)
                & (key_col <= col_start + 2 * REACH)
            )
            bias[b] = jnp.where(seen, 0.0, masked_score)
        def weigh(p):
            low, high = 16 * p, SHIFT + 16 * p
            here = pl.ds(128 * p, SPAN)
            there = pl.ds(512 + 128 * p, SPAN)
            query_turned = split_turned(query_all[j, pl.ds(at, 128), here], low)
            upward_turned = split_turned(upward_all[j, pl.ds(at, 128), here], high)
            scores = []
            for b in range(3):
                hidden = bias[b]
                scores.append(
                    mm(kv_ext[first_cb + b, band, here], query_turned)
                    + jnp.concatenate([hidden, hidden], axis=1)
                )
            top = functools.reduce(
                jnp.maximum, [jnp.max(x, axis=0, keepdims=True) for x in scores]
            )
            shifted = [jnp.exp2((x - top) * exp_scale) for x in scores]
            total = sum(jnp.sum(x, axis=0, keepdims=True) for x in shifted)
            inverse = 1.0 / total
            prob = [x * inverse for x in shifted]
            prob_low = [x.astype(bf16) for x in prob]
            dprob = [mm(kv_ext[first_cb + b, band, there], upward_turned) for b in range(3)]
            row_dot = sum(
                jnp.sum(x * y, axis=0, keepdims=True) for x, y in zip(prob, dprob)
            )
            dscore = [(x * (y - row_dot)).astype(bf16) for x, y in zip(prob, dprob)]
            return prob_low, dscore

        def spread(p, prob_low, dscore):
            low, high = 16 * p, SHIFT + 16 * p
            here = pl.ds(128 * p, SPAN)
            there = pl.ds(512 + 128 * p, SPAN)
            att = sum(mm(v_turned[p, first_cb + b, high : high + 2 * DH, band], prob_low[b]) for b in range(3))
            dquery = sum(mm(k_turned[p, first_cb + b, low : low + 2 * DH, band], dscore[b]) for b in range(3))
            rows = pl.ds(16 * t, 16)
            att_sum[rows, j, :, here] += joined(att, high)
            dq_sum[rows, j, :, here] += joined(dquery, low)
            query_rows = split_rows(query_all[j, pl.ds(at, 128), here], low)
            upward_rows = split_rows(upward_all[j, pl.ds(at, 128), here], high)
            for b in range(3):
                grads[first_cb + b, band, here] += mm(dscore[b], query_rows)
                grads[first_cb + b, band, there] += mm(prob_low[b], upward_rows)

        ready = weigh(0)
        for p in range(PAIRS):
            later = weigh(p + 1) if p + 1 < PAIRS else None
            spread(p, *ready)
            ready = later
        return 0

    lax.fori_loop(0, 4, strip, 0)
    scale = DH ** (-0.5)
    att_ref[...] = att_sum[...].reshape(att_ref.shape).astype(bf16)
    dq_ref[...] = (dq_sum[...] * scale).reshape(dq_ref.shape).astype(bf16)
    for cb in range(4):
        dkv_ref[cb, :, :INNER] = (grads[cb, :, :INNER] * scale).astype(bf16)
        dkv_ref[cb, :, INNER:] = grads[cb, :, INNER:].astype(bf16)

    for dc in (-1, 1):

        @pl.when(inside(row, col - dc))
        def _():
            sideways(2, dc).wait_send()

        for n in range(2):

            @pl.when(inside(row + 2 * n - 1, col) & inside(row, col - dc))
            def _():
                sideways(n, dc).wait_send()

    rows.wait_sends()


def front(token_rows, grad_rows, qkv_turned, out_turned):
    dma = pltpu.SemaphoreType.DMA
    frame_rows = 32 * lax.axis_size("row")
    frame_cols = 16 * lax.axis_size("col")
    tokens, width = token_rows.shape
    extended = (4, 384, width)
    return pl.pallas_call(
        functools.partial(front_kernel, frame_cols - WINDOW, frame_rows - WINDOW),
        out_shape=(
            jax.ShapeDtypeStruct(extended, bf16),
            jax.ShapeDtypeStruct((tokens, WIDE), bf16),
            jax.ShapeDtypeStruct((tokens, WIDE), bf16),
            jax.ShapeDtypeStruct(extended, bf16),
        ),
        in_specs=[ANY_SPEC] * 4,
        out_specs=(VMEM_SPEC,) * 4,
        scratch_shapes=[
            pltpu.VMEM(token_rows.shape, bf16),
            pltpu.VMEM(token_rows.shape, bf16),
            pltpu.VMEM(qkv_turned.shape, bf16),
            pltpu.VMEM(out_turned.shape, bf16),
            pltpu.VMEM((2, 64, 2 * INNER), bf16),
            pltpu.VMEM(extended, bf16),
            pltpu.VMEM((2, 256, WIDE), bf16),
            pltpu.VMEM((2, 256, WIDE), bf16),
            pltpu.VMEM(extended, f32),
            pltpu.VMEM((PAIRS, 4, SPAN, 384), bf16),
            pltpu.VMEM((PAIRS, 4, SPAN, 384), bf16),
            pltpu.VMEM((3, 256, 128), f32),
            pltpu.VMEM((32, 2, 8, WIDE), f32),
            pltpu.VMEM((32, 2, 8, WIDE), f32),
            dma((5,)),
            dma((2, 2)),
            dma((2, 2)),
            dma((2,)),
            dma((2,)),
            dma((2, 3)),
            dma((2, 3)),
        ],
        compiler_params=pltpu.CompilerParams(
            collective_id=0, has_side_effects=True, vmem_limit_bytes=51 * 2**20
        ),
        name="front",
    )(token_rows, grad_rows, qkv_turned, out_turned)


PIECES = [(0, 64), (320, 64), (64, 256)]
UPPER = 80
LOWER = 144 - UPPER


def tail_kernel(
    ext_ref, dkv_ref, dq_ref, att_ref, tok_hbm, up_hbm, wqkv_hbm, wout_hbm,
    out_ref, tokens_grad_ref, sublayer_ref, tok_ref, up_ref, wqkv_ref, wout_ref,
    side, up_down, flat, relay, total, dkv_own, turned, ext_turned,
    mine, theirs, recv0, rx1, ry1, a1, a2, rx2, ry2, b, rz, w, fin,
    load_sem, send_col, recv_col, send_row, recv_row, relay_send, relay_recv, sem0,
    sem_x1, sem_y1, sem_x2, sem_y2, send_z, recv_z, send_f, recv_f, local_sem,
):
    img = lax.axis_index("img")
    row, col = place()
    z_hi, y = row // 4, row % 4
    z_lo, core = col // 2, col % 2
    z = z_hi * 4 + z_lo
    other = 1 - core

    def device(img=img, z_hi=z_hi, y=y, z_lo=z_lo, core=core):
        return {"img": img, "row": z_hi * 4 + y, "col": z_lo * 2 + core}

    loads = [
        pltpu.make_async_copy(src, dst, load_sem.at[n])
        for n, (src, dst) in enumerate(
            ((up_hbm, up_ref), (tok_hbm, tok_ref), (wout_hbm, wout_ref), (wqkv_hbm, wqkv_ref))
        )
    ]
    for load in loads:
        load.start()
    barrier, count = greet(meets(row, col))
    greeted = [device(core=other)]
    greeted += [device(img=(img + d) % 4) for d in range(1, 4)]
    greeted += [device(img=(img + d) % 4, core=other) for d in range(1, 4)]
    greeted += [device(y=(y + d) % 4) for d in range(1, 4)]
    for d in range(1, 8):
        z_there = (z + d) % 8
        greeted.append(device(z_hi=z_there // 4, z_lo=z_there % 4))
    for target in greeted:
        pl.semaphore_signal(barrier, inc=1, device_id=target, device_id_type=MESH)
    pl.semaphore_wait(barrier, count + len(greeted))

    def to_side(k, piece):
        at = pl.ds(*PIECES[piece])
        return remote(
            dkv_ref.at[3 * k, at], side.at[k, at], send_col.at[k, piece], recv_col.at[k, piece],
            {"row": row, "col": col + 2 * k - 1},
        )

    def has_col(k):
        return inside(row, col + 2 * k - 1)

    def has_row(k):
        return inside(row + 2 * k - 1, col)

    for piece in range(3):
        for k in range(2):

            @pl.when(has_col(k))
            def _():
                to_side(k, piece).start()

    rows = RowExchange(
        row, col, lambda k, cb: up_down.at[k, cb], lambda k, cb: flat.at[k, cb],
        relay, send_row, recv_row, relay_send, relay_recv,
    )

    def gather(piece, cb):
        at = pl.ds(*PIECES[piece])
        total[cb, at] = dkv_ref[1 + cb, at].astype(f32)

        @pl.when(has_col(cb))
        def _():
            to_side(1 - cb, piece).wait_recv()
            total[cb, at] += side[1 - cb, at].astype(f32)

    def return_ends():
        for k in range(2):
            for cb in range(2):

                @pl.when(has_row(k))
                def _():
                    gather(k, cb)
                    up_down[k, cb] = total[cb, pl.ds(*PIECES[k])].astype(bf16)

                rows.start(k, cb)

                @pl.when(jnp.logical_not(has_row(k)) & has_col(cb))
                def _():
                    to_side(1 - cb, k).wait_recv()

    def weight_rows(half, n, group):
        at = pl.ds(pl.multiple_of(576 * half + 288 * n, 32), 288)
        if group == 3:
            grad = mm(turned[1, at], att_ref[...])
        elif group == 0:
            grad = mm(turned[0, at], dq_ref[...])
        else:
            lanes = pl.ds(0 if group == 1 else 2 * INNER - WIDE, WIDE)
            grad = mm(ext_turned[at], dkv_ref[:, :, lanes].reshape(1536, WIDE))
        return grad.reshape(2, 144, WIDE)

    def swap(n):
        at = pl.ds(2 * n, 2)
        return remote(
            theirs.at[at], recv0.at[at], sem0.at[0, n], sem0.at[1, n], device(core=other)
        )

    def for_pair(n):
        for group in range(4):
            theirs[2 * n : 2 * n + 2, group] = weight_rows(other, n, group).astype(bf16)
        swap(n).start()

    def for_self(n):
        swap(n).wait_recv()
        for group in range(4):
            at = slice(2 * n, 2 * n + 2)
            grad = weight_rows(core, n, group) + recv0[at, group].astype(f32)
            mine[at, group] = grad.astype(bf16)

    def over_x(d, n):
        x_there = (img + d) % 4
        at = pl.ds(2 * n, 2)
        return remote(
            mine.at[at, x_there, :UPPER], rx1.at[d - 1, at],
            sem_x1.at[0, d - 1, n], sem_x1.at[1, d - 1, n], device(img=x_there),
        )

    def over_y(d):
        y_there = (y + d) % 4
        return remote(
            mine.at[y_there, :, UPPER:], ry1.at[d - 1],
            sem_y1.at[0, d - 1], sem_y1.at[1, d - 1], device(y=y_there),
        )

    def send_first(n):
        for d in range(1, 4):
            over_x(d, n).start()

            @pl.when((y + d) % 4 // 2 == n)
            def _():
                over_y(d).start()

    def outward(n, _):
        at = pl.ds(pl.multiple_of(256 * n, 256), 256)
        sublayer_ref[at] = mm(att_ref[at, SHIFT:], wout_ref[...]).astype(bf16)
        return 0

    loads[0].wait()
    turned[1] = up_ref[...].T
    loads[1].wait()
    turned[0] = tok_ref[...].T
    for cb in range(4):
        ext_turned[:, pl.ds(384 * cb, 384)] = ext_ref[cb].T
    for_pair(0)
    return_ends()
    for_self(0)
    send_first(0)
    for_pair(1)
    rows.pass_on(False)
    loads[2].wait()
    lax.fori_loop(0, 2, outward, 0)
    for_self(1)
    send_first(1)
    rows.pass_on(True)

    def inward(n, _):
        at = pl.ds(pl.multiple_of(256 * n, 256), 256)
        grad = mm(dq_ref[at, :INNER], wqkv_ref[:INNER]) + mm(dkv_own[at], wqkv_ref[INNER:])
        tokens_grad_ref[at] = grad.astype(bf16)
        return 0

    for d in range(1, 4):
        over_x(d, 0).wait_recv()
        over_x(d, 1).wait_recv()
        over_y(d).wait_recv()

    def add_first(n, _):
        upper = mine[n, img, :UPPER].astype(f32)
        lower = mine[y, n, UPPER:].astype(f32)
        for d in range(3):
            upper += rx1[d, n].astype(f32)
            lower += ry1[d, n].astype(f32)
        a1[n] = upper.astype(bf16)
        a2[n] = lower.astype(bf16)
        return 0

    lax.fori_loop(0, 4, add_first, 0)

    second = []
    for d in range(1, 4):
        x_there, y_there = (img + d) % 4, (y + d) % 4
        second.append(
            remote(
                a1.at[y_there], ry2.at[d - 1],
                sem_y2.at[0, d - 1], sem_y2.at[1, d - 1], device(y=y_there),
            )
        )
        second.append(
            remote(
                a2.at[x_there], rx2.at[d - 1],
                sem_x2.at[0, d - 1], sem_x2.at[1, d - 1], device(img=x_there),
            )
        )
    for copy in second:
        copy.start()
    gather(2, 0)
    gather(2, 1)
    for copy in second:
        copy.wait_recv()
    upper = a1[y].astype(f32)
    lower = a2[img].astype(f32)
    for d in range(3):
        upper += ry2[d].astype(f32)
        lower += rx2[d].astype(f32)
    b[:UPPER] = upper.astype(bf16)
    b[UPPER:] = lower.astype(bf16)

    holder = z_hi == core

    def to_chip(n):
        return remote(
            b.at[pl.ds(32 * n, 48)], rz.at[z], send_z.at[n], recv_z.at[z],
            device(z_hi=core, z_lo=n),
        )

    def from_chip(n):
        return remote(
            b.at[pl.ds(0, 48)], rz.at[n], send_z.at[0], recv_z.at[n], device(core=other)
        )

    for n in range(4):

        @pl.when(jnp.logical_not(holder & (z_lo == n)))
        def _():
            to_chip(n).start()

    for k in range(2):

        @pl.when(has_row(1 - k))
        def _():
            first = 64 if k == 1 else 256
            for cb in range(2):
                rows.wait_recv(k, cb)
                total[cb, pl.ds(first, 64)] += flat[k, cb].astype(f32)

    owned = total[:, 64:320].reshape(2, 32, 8, 2 * INNER)
    dkv_own[...] = jnp.stack([owned[0], owned[1]], axis=1).reshape(dkv_own.shape).astype(bf16)
    loads[3].wait()
    lax.fori_loop(0, 2, inward, 0)

    def to_owner(d, k):
        return remote(
            w.at[pl.ds(16 * k, 32)], fin.at[img], send_f.at[d, k], recv_f.at[img],
            device(img=(img + d) % 4, core=k),
        )

    @pl.when(holder)
    def _():
        for n in range(8):

            @pl.when(z != n)
            def _():
                from_chip(n).wait_recv()

        own = b[pl.ds(pl.multiple_of(32 * z_lo, 32), 48)].astype(f32)
        rz[z] = own.astype(bf16)
        added = rz[0].astype(f32)
        for n in range(1, 8):
            added += rz[n].astype(f32)
        w[...] = added.astype(bf16)
        for d in range(4):
            for k in range(2):

                @pl.when((core != k) | (d != 0))
                def _():
                    to_owner(d, k).start()

        kept = pltpu.make_async_copy(
            w.at[pl.ds(pl.multiple_of(16 * core, 16), 32)], fin.at[img], local_sem.at[4]
        )
        kept.start()
        kept.wait()

    def from_holder(n):
        return remote(
            w.at[pl.ds(0, 32)], fin.at[n], send_f.at[0, 0], recv_f.at[n], device(core=other)
        )

    for n in range(4):

        @pl.when(jnp.logical_not(holder) | (img != n))
        def _():
            from_holder(n).wait_recv()

    out_ref[...] = fin[...]

    rows.wait_sends()
    for k in range(2):

        @pl.when(has_col(k))
        def _():
            for piece in range(3):
                to_side(k, piece).wait_send()

    for d in range(1, 4):
        over_x(d, 0).wait_send()
        over_x(d, 1).wait_send()
        over_y(d).wait_send()
    for n in range(2):
        swap(n).wait_send()
    for copy in second:
        copy.wait_send()
    for n in range(4):

        @pl.when(jnp.logical_not(holder & (z_lo == n)))
        def _():
            to_chip(n).wait_send()

    @pl.when(holder)
    def _():
        for d in range(4):
            for k in range(2):

                @pl.when((core != k) | (d != 0))
                def _():
                    to_owner(d, k).wait_send()


def tail(ext, dkv, dq, att, token_rows, grad_rows, qkv_turned, out_turned):
    dma = pltpu.SemaphoreType.DMA
    tokens, width = token_rows.shape
    return pl.pallas_call(
        tail_kernel,
        out_shape=(
            jax.ShapeDtypeStruct((4, 32, WIDE), bf16),
            jax.ShapeDtypeStruct(token_rows.shape, bf16),
            jax.ShapeDtypeStruct(token_rows.shape, bf16),
        ),
        in_specs=[VMEM_SPEC] * 4 + [ANY_SPEC] * 4,
        out_specs=(VMEM_SPEC,) * 3,
        scratch_shapes=[
            pltpu.VMEM(token_rows.shape, bf16),
            pltpu.VMEM(token_rows.shape, bf16),
            pltpu.VMEM(qkv_turned.shape, bf16),
            pltpu.VMEM(out_turned.shape, bf16),
            pltpu.VMEM((2, 384, 2 * INNER), bf16),
            pltpu.VMEM((2, 2, 64, 2 * INNER), bf16),
            pltpu.VMEM((2, 2, 64, 2 * INNER), bf16),
            pltpu.VMEM((2, 64, 2 * INNER), bf16),
            pltpu.VMEM((2, 384, 2 * INNER), f32),
            pltpu.VMEM((tokens, 2 * INNER), bf16),
            pltpu.VMEM((2, width, tokens), bf16),
            pltpu.VMEM((width, 4 * 384), bf16),
            pltpu.VMEM((4, 4, 144, WIDE), bf16),
            pltpu.VMEM((4, 4, 144, WIDE), bf16),
            pltpu.VMEM((4, 4, 144, WIDE), bf16),
            pltpu.VMEM((3, 4, UPPER, WIDE), bf16),
            pltpu.VMEM((3, 4, LOWER, WIDE), bf16),
            pltpu.VMEM((4, UPPER, WIDE), bf16),
            pltpu.VMEM((4, LOWER, WIDE), bf16),
            pltpu.VMEM((3, LOWER, WIDE), bf16),
            pltpu.VMEM((3, UPPER, WIDE), bf16),
            pltpu.VMEM((144, WIDE), bf16),
            pltpu.VMEM((8, 48, WIDE), bf16),
            pltpu.VMEM((48, WIDE), bf16),
            pltpu.VMEM((4, 32, WIDE), bf16),
            dma((4,)),
            dma((2, 3)),
            dma((2, 3)),
            dma((2, 2)),
            dma((2, 2)),
            dma((2,)),
            dma((2,)),
            dma((2, 2)),
            dma((2, 3, 2)),
            dma((2, 3)),
            dma((2, 3)),
            dma((2, 3)),
            dma((4,)),
            dma((8,)),
            dma((4, 2)),
            dma((4,)),
            dma((5,)),
        ],
        compiler_params=pltpu.CompilerParams(
            collective_id=1, has_side_effects=True, vmem_limit_bytes=50 * 2**20
        ),
        name="tail",
    )(ext, dkv, dq, att, token_rows, grad_rows, qkv_turned, out_turned)


def local(tokens, qkv_weight, out_weight, upstream):
    count = tokens.shape[1] * tokens.shape[2]
    width = tokens.shape[3]
    token_rows = tokens.reshape(count, width)
    grad_rows = upstream.reshape(count, width)
    qkv_turned, out_turned = qkv_weight.T, out_weight.T
    extended, att, dq, dkv = front(token_rows, grad_rows, qkv_turned, out_turned)
    shares, tokens_grad, sublayer_out = tail(
        extended, dkv, dq, att, token_rows, grad_rows, qkv_turned, out_turned
    )
    shares = lax.dynamic_slice_in_dim(shares, 2 * lax.axis_index("col"), 18, 1).astype(f32)
    qkv_grad = jnp.concatenate(
        [shares[0, :, :INNER], shares[1, :, :INNER], shares[2, :, SHIFT:]], axis=1
    )
    return (
        sublayer_out.reshape(tokens.shape),
        tokens_grad.reshape(tokens.shape),
        qkv_grad,
        shares[3, :, SHIFT:],
    )


def solution(mesh):
    return jax.shard_map(
        local,
        mesh=mesh,
        in_specs=(P("img", "row", "col", None), P(), P(), P("img", "row", "col", None)),
        out_specs=(
            P("img", "row", "col", None),
            P("img", "row", "col", None),
            P(("row", "col"), None),
            P(("row", "col"), None),
        ),
        check_vma=False,
    )
```
